1024 devices in a mesh: dp: 32 (over y, z_hi), blk: 32 (over z_lo, x, core).
Axes of the slice: x: 4, y: 8, z: 16 (z_hi: 4, z_lo: 4; z = z_hi * 4 + z_lo), core: 2. Of those that a mesh axis runs over, the one named last changes fastest.
Arguments:
- captions: bfloat16 [32, 32, 24, 16, 1152], P('dp', 'blk')
- lengths: int32 [32, 32, 24], P('dp', 'blk'), may hold values from 4 to 16, as said below
- destination: int32 [32, 32, 24], P('dp', 'blk'), may hold values from 0 to 31, as said below
- labels: int32 [32, 32, 24], P('dp', 'blk'), may hold values from 0 to 1023
- images: bfloat16 [32, 32, 32, 1152], P('dp', 'blk')
- position: bfloat16 [16, 1152], replicated, may hold values from -6 to 6
- gain_in: float32 [1152], replicated, may hold values from 0.4 to 2.5
- gain_out: float32 [1152], replicated, may hold values from 0.4 to 2.5
- query_proj: bfloat16 [1152, 576], replicated, may hold values from -0.1875 to 0.1875
- pair_proj: bfloat16 [1152, 1152], replicated, may hold values from -0.1875 to 0.1875
- out_proj: bfloat16 [576, 1152], replicated, may hold values from -0.25 to 0.25
- head_proj: bfloat16 [1152, 1152], replicated, may hold values from -0.1875 to 0.1875
- temper: float32 [8], replicated, may hold values from 3 to 12
- logit_scale: float32 [1], replicated, may hold values from 4 to 12
- logit_bias: float32 [1], replicated, may hold values from -3 to -0.5
Outputs:
- text_grad: float32 [32, 32, 32, 1152], P('dp', 'blk')
- image_grad: float32 [32, 32, 32, 1152], P('dp', 'blk')
The draws below stay inside these ranges and needn't reach their ends.
Inputs may be any that keep to these rules, and one draw needn't show every extreme that they name: The 24 rows of one device name different destinations; in each blk column one destination receives a row from every dp index, so at most one caption goes from one device to one destination. `lengths`: positions at and after a row's count are padding. `labels`: the paired image's row among the 1024 images of the destination's dp index, ordered by blk index and then by row.
All inputs are finite; a program needn't handle non-finite values.
Results may differ from the reference program's by a relative error of at most 0.0095.
Values may be sent and summed in bfloat16 or wider, within the bound.
No kernel may reach another device: no remote copies, remote signals or barrier semaphores. Data moves between devices by JAX's collectives and lax.ppermute only.
A program may use at most 64 MiB of HBM per device.

```python
import math
import jax
import jax.numpy as jnp
from jax import lax

D = 1152
HSZ = 72
HEADS = 8
LEN = 16
IMG = 32
ROWS = 24
N_DP = 32
N_BLK = 32


def route_plan(key):
    first, second, third, fourth = jax.random.split(key, 4)
    hottest = jax.random.randint(first, (N_BLK,), 0, N_DP)
    places = jnp.arange(N_DP, dtype=jnp.int32)
    score = jax.random.randint(second, (N_DP, N_BLK, N_DP), 0, 1048576) * N_DP + places
    score = score + jnp.where(places[None, None, :] == hottest[None, :, None], 67108864, 0)
    picked = jax.lax.top_k(score, ROWS)[1]
    shuffle = jax.random.randint(third, (N_DP, N_BLK, ROWS), 0, 1048576) * ROWS + jnp.arange(ROWS, dtype=jnp.int32)
    order = jax.lax.top_k(shuffle, ROWS)[1]
    picked = jnp.take_along_axis(picked, order, axis=2).astype(jnp.int32)
    counts = jax.random.randint(fourth, (N_DP, N_BLK, ROWS), (LEN + 4) // 5, LEN)
    counts = jnp.where(picked == hottest[None, :, None], LEN, counts).astype(jnp.int32)
    return (picked, counts)


def draw_destination(key, part):
    return route_plan(key)[0]


def draw_lengths(key, part):
    return route_plan(key)[1]


def draw_captions(key, part):
    key = jax.random.fold_in(key, 7)
    first, second, third = jax.random.split(key, 3)
    shape = (N_DP, N_BLK, ROWS, LEN, D)
    base = jax.random.normal(first, shape, jnp.float32)
    top = math.log(10.0)
    row_scale = jnp.exp(jax.random.uniform(second, shape[:-1] + (1,), jnp.float32, 0.0, top))
    column_scale = jnp.exp(jax.random.uniform(third, (D,), jnp.float32, 0.0, top))
    return (base * row_scale * column_scale).astype(jnp.bfloat16)


def draw_images(key, part):
    key = jax.random.fold_in(key, 9)
    first, second, third = jax.random.split(key, 3)
    shape = (N_DP, N_BLK, IMG, D)
    base = jax.random.normal(first, shape, jnp.float32)
    top = math.log(10.0)
    row_scale = jnp.exp(jax.random.uniform(second, shape[:-1] + (1,), jnp.float32, 0.0, top))
    column_scale = jnp.exp(jax.random.uniform(third, (D,), jnp.float32, 0.0, top))
    return (base * row_scale * column_scale).astype(jnp.bfloat16)


def touch_ends(entries, key, low, largest):
    index_at = [jax.random.randint(jax.random.fold_in(key, axis), (), 0, length) for axis, length in enumerate(entries.shape)]
    widest = entries.shape.index(max(entries.shape))
    neighbour = index_at[:widest] + [(index_at[widest] + 1) % entries.shape[widest]] + index_at[widest + 1:]
    return entries.at[tuple(index_at)].set(low).at[tuple(neighbour)].set(largest)


def scatter_about(key, extent, width, reach, kind=jnp.bfloat16):
    return jnp.clip(width * jax.random.normal(key, extent, jnp.float32), -reach, reach).astype(kind)


def setup_inputs(seed: int = 0) -> dict:
    key_list = jax.random.split(jax.random.key(seed), 16)
    return {
        "captions": draw_captions(jax.random.fold_in(key_list[15], 71), 0),
        "lengths": draw_lengths(jax.random.fold_in(key_list[15], 71), 0),
        "destination": draw_destination(jax.random.fold_in(key_list[15], 71), 0),
        "labels": touch_ends(jax.random.randint(key_list[3], (N_DP, N_BLK, ROWS), 0, N_BLK * IMG), jax.random.fold_in(key_list[3], 1), 0, (N_BLK * IMG) - 1).astype(jnp.int32),
        "images": draw_images(jax.random.fold_in(key_list[15], 71), 0),
        "position": scatter_about(key_list[5], (LEN, D), 1.0, 6.0),
        "gain_in": jnp.clip(jnp.exp(jax.random.uniform(key_list[6], (D,), jnp.float32, math.log(0.4), math.log(2.5))), 0.4, 2.5),
        "gain_out": jnp.clip(jnp.exp(jax.random.uniform(key_list[7], (D,), jnp.float32, math.log(0.4), math.log(2.5))), 0.4, 2.5),
        "query_proj": scatter_about(key_list[8], (D, HEADS * HSZ), D ** -0.5, 0.1875),
        "pair_proj": scatter_about(key_list[9], (D, 2 * HEADS * HSZ), D ** -0.5, 0.1875),
        "out_proj": scatter_about(key_list[10], (HEADS * HSZ, D), (HEADS * HSZ) ** -0.5, 0.25),
        "head_proj": scatter_about(key_list[11], (D, D), D ** -0.5, 0.1875),
        "temper": jnp.clip(jnp.exp(jax.random.uniform(key_list[12], (HEADS,), jnp.float32, math.log(3.0), math.log(12.0))), 3.0, 12.0),
        "logit_scale": jnp.clip(jnp.exp(jax.random.uniform(key_list[13], (1,), jnp.float32, math.log(4.0), math.log(12.0))), 4.0, 12.0),
        "logit_bias": jnp.clip(jax.random.uniform(key_list[14], (1,), jnp.float32, -3.0, -0.5), -3.0, -0.5),
    }


def layer_norm(values, gain):
    center = values - lax.optimization_barrier(jnp.mean(values, axis=-1, keepdims=True))
    spread = lax.optimization_barrier(jnp.mean(center * center, axis=-1, keepdims=True))
    return center * lax.rsqrt(spread + 1e-06) * gain

def unit_rows(values):
    return values * lax.rsqrt(lax.optimization_barrier(jnp.sum(values * values, axis=-1, keepdims=True)) + 1e-06)

def text_tower(tokens, counts, position, gain_in, gain_out, query_proj, pair_proj, out_proj, head_proj, temper):
    number = tokens.shape[0]
    summed = tokens.astype(jnp.float32) + position.astype(jnp.float32)[None]
    normed = layer_norm(summed, gain_in).astype(jnp.bfloat16)
    paired = jnp.dot(normed.reshape(number * LEN, D), pair_proj, preferred_element_type=jnp.float32).astype(jnp.bfloat16)
    paired = paired.reshape(number, LEN, 2, HEADS, HSZ)
    bounded = jnp.maximum(counts, 1).astype(jnp.int32)
    final_pos = (bounded - 1)[:, None, None]
    normed_last = jnp.take_along_axis(normed, final_pos, axis=1)[:, 0]
    summed_last = jnp.take_along_axis(summed, final_pos, axis=1)[:, 0]
    queries = jnp.dot(normed_last, query_proj, preferred_element_type=jnp.float32).reshape(number, HEADS, HSZ)
    query_unit = unit_rows(queries) * temper[None, :, None]
    key_unit = unit_rows(paired[:, :, 0].astype(jnp.float32))
    scores = jnp.einsum('chs,clhs->chl', query_unit, key_unit)
    visible = jnp.arange(LEN, dtype=jnp.int32)[None, :] < bounded[:, None]
    raised = jnp.where(visible[:, None, :], jnp.exp(scores), 0.0)
    probs = (raised / lax.optimization_barrier(jnp.sum(raised, axis=2, keepdims=True))).astype(jnp.bfloat16)
    attended = jnp.einsum('chl,clhs->chs', probs.astype(jnp.float32), paired[:, :, 1].astype(jnp.float32))
    attended = attended.astype(jnp.bfloat16).reshape(number, HEADS * HSZ)
    residual_out = summed_last + jnp.dot(attended, out_proj, preferred_element_type=jnp.float32)
    final_normed = layer_norm(residual_out, gain_out).astype(jnp.bfloat16)
    return unit_rows(jnp.dot(final_normed, head_proj, preferred_element_type=jnp.float32)).astype(jnp.bfloat16)

def reference(captions, lengths, destination, labels, images, position, gain_in, gain_out, query_proj, pair_proj, out_proj, head_proj, temper, logit_scale, logit_bias):
    flat_captions = captions.reshape(N_DP, N_BLK * ROWS, LEN, D)
    flat_counts = lengths.reshape(N_DP, N_BLK * ROWS)

    def encode(pack):
        return text_tower(pack[0], pack[1], position, gain_in, gain_out, query_proj, pair_proj, out_proj, head_proj, temper)
    pooled = lax.map(encode, (flat_captions, flat_counts)).reshape(N_DP, N_BLK, ROWS, D)
    routing = (destination[..., None] == jnp.arange(N_DP, dtype=jnp.int32)).astype(jnp.int32)
    paired_text = jnp.einsum('sbrd,sbrk->dbsk', routing.astype(jnp.float32), pooled.astype(jnp.float32)).astype(jnp.bfloat16)
    live = jnp.transpose(lax.optimization_barrier(jnp.sum(routing, axis=2)), (2, 1, 0))
    slot_label = jnp.transpose(lax.optimization_barrier(jnp.sum(routing * labels[..., None], axis=2)), (2, 1, 0))
    image_unit = unit_rows(images.astype(jnp.float32)).astype(jnp.bfloat16)
    scale = logit_scale[0]
    offset = logit_bias[0]
    image_index = jnp.arange(N_BLK * IMG, dtype=jnp.int32)

    def group(pack):
        text_rows = pack[0].reshape(N_BLK * N_DP, D)
        text_label = pack[1].reshape(N_BLK * N_DP)
        text_live = pack[2].reshape(N_BLK * N_DP)
        image_rows = pack[3].reshape(N_BLK * IMG, D)
        logits = scale * jnp.dot(text_rows, image_rows.T, preferred_element_type=jnp.float32) + offset
        sign = jnp.where(text_label[:, None] == image_index[None, :], 1.0, -1.0)
        slopes = (-sign / (1.0 + jnp.exp(sign * logits)) * text_live[:, None].astype(jnp.float32)).astype(jnp.bfloat16)
        text_part = scale * jnp.dot(slopes, image_rows, preferred_element_type=jnp.float32)
        image_part = scale * jnp.dot(slopes.T, text_rows, preferred_element_type=jnp.float32)
        return (text_part, image_part)
    text_grad, image_grad = lax.map(group, (paired_text, slot_label, live, image_unit))
    return (text_grad.reshape(N_DP, N_BLK, N_DP, D), image_grad.reshape(N_DP, N_BLK, IMG, D))
```

```python
import jax
import jax.numpy as jnp
from jax import lax
from jax.sharding import PartitionSpec as P

CS = 2
XS = 4
AUX = 128


def layer_norm(values, gain):
    center = values - jnp.mean(values, axis=-1, keepdims=True)
    spread = jnp.mean(center * center, axis=-1, keepdims=True)
    return center * lax.rsqrt(spread + 1e-06) * gain


def unit_rows(values):
    return values * lax.rsqrt(jnp.sum(values * values, axis=-1, keepdims=True) + 1e-06)


def text_tower(tokens, counts, params):
    position, gain_in, gain_out, query_proj, pair_proj, out_proj, head_proj, temper = params
    number = tokens.shape[0]
    length = tokens.shape[1]
    width = tokens.shape[2]
    heads = temper.shape[0]
    head_size = query_proj.shape[1] // heads
    summed = tokens.astype(jnp.float32) + position.astype(jnp.float32)[None]
    normed = layer_norm(summed, gain_in).astype(jnp.bfloat16)
    paired = jnp.dot(
        normed.reshape(number * length, width), pair_proj, preferred_element_type=jnp.float32
    ).astype(jnp.bfloat16)
    paired = paired.reshape(number, length, 2, heads, head_size)
    bounded = jnp.maximum(counts, 1)
    final_pos = (bounded - 1)[:, None, None]
    normed_last = jnp.take_along_axis(normed, final_pos, axis=1)[:, 0]
    summed_last = jnp.take_along_axis(summed, final_pos, axis=1)[:, 0]
    queries = jnp.dot(normed_last, query_proj, preferred_element_type=jnp.float32).reshape(
        number, heads, head_size
    )
    query_unit = unit_rows(queries) * temper[None, :, None]
    key_unit = unit_rows(paired[:, :, 0].astype(jnp.float32))
    scores = jnp.einsum("chs,clhs->chl", query_unit, key_unit)
    visible = jnp.arange(length, dtype=jnp.int32)[None, :] < bounded[:, None]
    raised = jnp.where(visible[:, None, :], jnp.exp(scores), 0.0)
    probs = (raised / jnp.sum(raised, axis=2, keepdims=True)).astype(jnp.bfloat16)
    attended = jnp.einsum(
        "chl,clhs->chs", probs, paired[:, :, 1], preferred_element_type=jnp.float32
    )
    attended = attended.astype(jnp.bfloat16).reshape(number, heads * head_size)
    residual_out = summed_last + jnp.dot(attended, out_proj, preferred_element_type=jnp.float32)
    final_normed = layer_norm(residual_out, gain_out).astype(jnp.bfloat16)
    return unit_rows(jnp.dot(final_normed, head_proj, preferred_element_type=jnp.float32)).astype(
        jnp.bfloat16
    )


def encode(captions, counts, target, label, params, slots):
    text = text_tower(captions, counts, params)
    number = text.shape[0]
    column = jnp.arange(AUX, dtype=jnp.int32)[None, :]
    high = (label // 32)[:, None]
    low = (label % 32)[:, None]
    aux = jnp.where(column == 0, high, jnp.where(column == 1, low, jnp.where(column == 2, 1, 0)))
    wide = jnp.concatenate([text, aux.astype(jnp.bfloat16)], axis=1)
    routing = (target[None, :] == jnp.arange(slots, dtype=jnp.int32)[:, None]).astype(jnp.bfloat16)
    return jnp.dot(routing, wide, preferred_element_type=jnp.float32).astype(jnp.bfloat16)


def slope_of(logits, same, live):
    sign = jnp.where(same, 1.0, -1.0)
    return (-sign / (1.0 + jnp.exp(sign * logits)) * live).astype(jnp.bfloat16)


NT = (((1,), (1,)), ((), ()))


def text_part(wide, image_all, scale, offset):
    width = image_all.shape[1]
    text = wide[:, :width]
    aux = wide[:, width:].astype(jnp.float32)
    label = aux[:, 0:1] * 32.0 + aux[:, 1:2]
    live = aux[:, 2:3]
    logits = scale * lax.dot_general(text, image_all, NT, preferred_element_type=jnp.float32) + offset
    index = jnp.arange(image_all.shape[0], dtype=jnp.int32)[None, :].astype(jnp.float32)
    slopes = slope_of(logits, label == index, live)
    return scale * jnp.dot(slopes, image_all, preferred_element_type=jnp.float32)


def image_parts(wide, images, index, scale, offset):
    width = images.shape[1]
    text = wide[:, :width]
    aux = wide[:, width:].astype(jnp.float32)
    label = (aux[:, 0] * 32.0 + aux[:, 1])[None, :]
    live = aux[:, 2][None, :]
    logits = scale * lax.dot_general(images, text, NT, preferred_element_type=jnp.float32) + offset
    slopes = slope_of(logits, label == index[:, None].astype(jnp.float32), live)
    return scale * jnp.dot(slopes, text, preferred_element_type=jnp.float32)


def loss_grads(wide, image_unit, image_all, scale, offset):
    blocks = lax.axis_size("blk")
    zs = blocks // (XS * CS)
    count, width = image_unit.shape
    place = lambda z, x, c: (z * XS + x) * CS + c
    pairs = [[place(z, x, c) for c in range(CS)] for z in range(zs) for x in range(XS)]
    lines = [[place(z, x, c) for z in range(zs)] for x in range(XS) for c in range(CS)]
    gathered = lax.all_gather(wide, "blk", axis=0, tiled=True, axis_index_groups=pairs)
    gathered = lax.all_gather(gathered, "blk", axis=0, tiled=True, axis_index_groups=lines)
    mine = lax.axis_index("blk")
    my_x = (mine // CS) % XS
    base = mine - my_x * CS
    rows = []
    index = []
    for k in range(XS):
        there = base + ((my_x + k) % XS) * CS
        rows.append(lax.dynamic_slice_in_dim(image_all, there * count, count, axis=0))
        index.append(there * count + jnp.arange(count, dtype=jnp.int32))
    parts = image_parts(
        gathered, jnp.concatenate(rows), jnp.concatenate(index), scale, offset
    ).reshape(XS, count, width)
    image_sum = parts[0]
    for k in range(1, XS):
        shift = [
            (place(z, x, c), place(z, (x + k) % XS, c))
            for z in range(zs)
            for x in range(XS)
            for c in range(CS)
        ]
        image_sum = image_sum + lax.ppermute(
            parts[k].astype(jnp.bfloat16), "blk", shift
        ).astype(jnp.float32)
    text_sum = text_part(wide, image_all, scale, offset)
    return text_sum, image_sum


def local(
    captions,
    lengths,
    destination,
    labels,
    images,
    position,
    gain_in,
    gain_out,
    query_proj,
    pair_proj,
    out_proj,
    head_proj,
    temper,
    logit_scale,
    logit_bias,
):
    slots = lax.axis_size("dp")
    params = (position, gain_in, gain_out, query_proj, pair_proj, out_proj, head_proj, temper)
    image_unit = unit_rows(images[0, 0].astype(jnp.float32)).astype(jnp.bfloat16)
    image_all = lax.all_gather(image_unit, "blk", axis=0, tiled=True)
    sent = encode(captions[0, 0], lengths[0, 0], destination[0, 0], labels[0, 0], params, slots)
    wide = lax.all_to_all(sent, "dp", split_axis=0, concat_axis=0, tiled=True)
    text_sum, image_sum = loss_grads(wide, image_unit, image_all, logit_scale[0], logit_bias[0])
    return text_sum[None, None], image_sum[None, None]


def solution(mesh):
    return jax.shard_map(
        local,
        mesh=mesh,
        in_specs=(
            P("dp", "blk", None, None, None),
            P("dp", "blk", None),
            P("dp", "blk", None),
            P("dp", "blk", None),
            P("dp", "blk", None, None),
            P(),
            P(),
            P(),
            P(),
            P(),
            P(),
            P(),
            P(),
            P(),
            P(),
        ),
        out_specs=(P("dp", "blk", None, None), P("dp", "blk", None, None)),
        check_vma=False,
    )
```

```python
import jax
import jax.numpy as jnp
from jax import lax
from jax.experimental import pallas as pl
from jax.experimental.pallas import tpu as pltpu
from jax.sharding import PartitionSpec as P

CS = 2
XS = 4
LANES = 128
AUX = 128
BATCHES = 8
CHUNKS = 4
NT = (((1,), (1,)), ((), ()))
TN = (((0,), (0,)), ((), ()))


def layer_norm(values, gain):
    center = values - jnp.mean(values, axis=-1, keepdims=True)
    spread = jnp.mean(center * center, axis=-1, keepdims=True)
    return center * lax.rsqrt(spread + 1e-06) * gain


def unit_rows(values):
    return values * lax.rsqrt(jnp.sum(values * values, axis=-1, keepdims=True) + 1e-06)


def split_dot(values, right, dims=(((1,), (0,)), ((), ()))):
    high = values.astype(jnp.bfloat16)
    low = (values - high.astype(jnp.float32)).astype(jnp.bfloat16)
    return lax.dot_general(high, right, dims, preferred_element_type=jnp.float32) + lax.dot_general(
        low, right, dims, preferred_element_type=jnp.float32
    )


def as_half(mask):
    return jnp.where(mask, 1.0, 0.0).astype(jnp.bfloat16)


def iota(shape, dimension):
    return lax.broadcasted_iota(jnp.int32, shape, dimension)


def tower_kernel(
    temper_ref,
    count_hbm,
    target_hbm,
    label_hbm,
    caption_hbm,
    position_hbm,
    gain_in_hbm,
    gain_out_hbm,
    query_hbm,
    pair_hbm,
    out_hbm,
    head_hbm,
    wide_ref,
    count_ref,
    target_ref,
    label_ref,
    caption_ref,
    position_ref,
    gain_in_ref,
    gain_out_ref,
    query_ref,
    pair_ref,
    out_ref,
    head_ref,
    normed_ref,
    kv_ref,
    sems,
):
    number, length, width = caption_ref.shape
    tokens = number * length
    inner = query_hbm.shape[0]
    heads = temper_ref.shape[0]
    size = inner // heads
    lead = out_ref.shape[0] - inner
    slots = wide_ref.shape[0]
    pair_copy = pltpu.make_async_copy(pair_hbm, pair_ref, sems.at[0])
    query_copy = pltpu.make_async_copy(query_hbm, query_ref, sems.at[1])
    out_copy = pltpu.make_async_copy(out_hbm, out_ref.at[pl.ds(lead, inner), :], sems.at[2])
    head_copy = pltpu.make_async_copy(head_hbm, head_ref, sems.at[3])
    group = number // BATCHES
    position_copy = pltpu.make_async_copy(position_hbm, position_ref, sems.at[4])
    gain_in_copy = pltpu.make_async_copy(gain_in_hbm, gain_in_ref, sems.at[5])
    gain_out_copy = pltpu.make_async_copy(gain_out_hbm, gain_out_ref, sems.at[6])
    count_copy = pltpu.make_async_copy(count_hbm, count_ref, sems.at[7])
    target_copy = pltpu.make_async_copy(target_hbm, target_ref, sems.at[8])
    label_copy = pltpu.make_async_copy(label_hbm, label_ref, sems.at[9])
    caption_copies = [
        pltpu.make_async_copy(
            caption_hbm.at[pl.ds(batch * group, group)],
            caption_ref.at[pl.ds(batch * group, group)],
            sems.at[10 + batch],
        )
        for batch in range(BATCHES)
    ]
    position_copy.start()
    gain_in_copy.start()
    for copy in caption_copies:
        copy.start()
    pair_copy.start()
    count_copy.start()
    label_copy.start()
    query_copy.start()
    out_copy.start()
    target_copy.start()
    gain_out_copy.start()
    head_copy.start()
    out_ref[0:lead, :] = jnp.zeros((lead, width), jnp.bfloat16)

    position_copy.wait()
    gain_in_copy.wait()
    gain_in = gain_in_ref[...]
    position = position_ref[...].astype(jnp.float32)
    for batch in range(BATCHES):
        start = batch * group
        caption_copies[batch].wait()
        summed = caption_ref[start : start + group].astype(jnp.float32) + position[None]
        normed = layer_norm(summed, gain_in[None]).astype(jnp.bfloat16)
        normed_ref[start * length : (start + group) * length, :] = normed.reshape(
            group * length, width
        )

    count_copy.wait()
    label_copy.wait()
    count_row = jnp.maximum(count_ref[...], 1).astype(jnp.float32)
    label_row = label_ref[...].astype(jnp.float32)
    diagonal = iota((number, number), 0) == iota((number, number), 1)
    count_col = jnp.sum(jnp.where(diagonal, count_row, 0.0), axis=1, keepdims=True)
    label_col = jnp.sum(jnp.where(diagonal, label_row, 0.0), axis=1, keepdims=True)
    last_col = count_col.astype(jnp.int32) - 1
    pick = as_half(iota((number, tokens), 1) == iota((number, tokens), 0) * length + last_col)
    pick_position = as_half(iota((number, length), 1) == last_col)
    member = as_half(iota((number, tokens), 1) // length == iota((number, tokens), 0))
    owner = iota((tokens, number), 0) // length == iota((tokens, number), 1)
    spread = as_half(owner)
    count_tok = jnp.sum(jnp.where(owner, count_row, 0.0), axis=1, keepdims=True)
    place_tok = (iota((tokens, 1), 0) % length).astype(jnp.float32)
    first = iota((inner, LANES), 1) * size
    key_heads = as_half((iota((inner, LANES), 0) >= first) & (iota((inner, LANES), 0) < first + size))
    wide_inner = lead + inner
    first = iota((LANES, wide_inner), 0) * size + lead
    value_heads = as_half(
        (iota((LANES, wide_inner), 1) >= first) & (iota((LANES, wide_inner), 1) < first + size)
    )
    lane = iota((1, LANES), 1)
    temper = jnp.zeros((1, LANES), jnp.float32)
    for head in range(heads):
        temper = jnp.where(lane == head, temper_ref[head], temper)

    pair_copy.wait()
    step = width // 3
    for start in range(0, width, step):
        kv_ref[:, start : start + step] = jnp.dot(
            normed_ref[...], pair_ref[:, start : start + step], preferred_element_type=jnp.float32
        ).astype(jnp.bfloat16)
    normed_last = jnp.dot(pick, normed_ref[...], preferred_element_type=jnp.float32).astype(
        jnp.bfloat16
    )
    flat = caption_ref[...].reshape(tokens, width)
    summed_last = jnp.dot(pick, flat, preferred_element_type=jnp.float32) + jnp.dot(
        pick_position, position_ref[...], preferred_element_type=jnp.float32
    )
    query_copy.wait()
    queries = lax.dot_general(
        normed_last, query_ref[...], NT, preferred_element_type=jnp.float32
    )
    query_norm = temper * lax.rsqrt(split_dot(queries * queries, key_heads) + 1e-06)
    query_high = queries.astype(jnp.bfloat16)
    query_low = (queries - query_high.astype(jnp.float32)).astype(jnp.bfloat16)
    norm_high = query_norm.astype(jnp.bfloat16)
    norm_low = (query_norm - norm_high.astype(jnp.float32)).astype(jnp.bfloat16)

    attended = jnp.zeros((number, wide_inner), jnp.float32)
    parts = 2
    some = tokens // parts
    for part in range(parts):
        rows = slice(part * some, (part + 1) * some)
        spread_part = spread[rows]
        query_tok = jnp.dot(
            spread_part, query_high, preferred_element_type=jnp.float32
        ) + jnp.dot(spread_part, query_low, preferred_element_type=jnp.float32)
        norm_tok = jnp.dot(
            spread_part, norm_high, preferred_element_type=jnp.float32
        ) + jnp.dot(spread_part, norm_low, preferred_element_type=jnp.float32)
        keys = kv_ref[rows, 0:inner].astype(jnp.float32)
        products = split_dot(keys * query_tok, key_heads)
        key_square = split_dot(keys * keys, key_heads)
        scores = products * lax.rsqrt(key_square + 1e-06) * norm_tok
        raised = jnp.where(place_tok[rows] < count_tok[rows], jnp.exp(scores), 0.0)
        raised = raised.reshape(some // length, length, LANES)
        probs = raised / jnp.sum(raised, axis=1, keepdims=True)
        probs = probs.reshape(some, LANES).astype(jnp.bfloat16)
        probs_wide = jnp.dot(probs, value_heads, preferred_element_type=jnp.float32)
        values = kv_ref[rows, width - wide_inner : width].astype(jnp.float32)
        weighed = probs_wide * values
        high = weighed.astype(jnp.bfloat16)
        low = (weighed - high.astype(jnp.float32)).astype(jnp.bfloat16)
        attended = (
            attended
            + jnp.dot(member[:, rows], high, preferred_element_type=jnp.float32)
            + jnp.dot(member[:, rows], low, preferred_element_type=jnp.float32)
        )
    out_copy.wait()
    residual = summed_last + jnp.dot(
        attended.astype(jnp.bfloat16), out_ref[...], preferred_element_type=jnp.float32
    )
    gain_out_copy.wait()
    final = layer_norm(residual, gain_out_ref[...]).astype(jnp.bfloat16)
    head_copy.wait()
    pooled = unit_rows(jnp.dot(final, head_ref[...], preferred_element_type=jnp.float32)).astype(
        jnp.bfloat16
    )
    target_copy.wait()
    route = as_half(target_ref[...] == iota((slots, number), 0))
    wide_ref[:, 0:width] = jnp.dot(route, pooled, preferred_element_type=jnp.float32).astype(
        jnp.bfloat16
    )
    label_int = label_col.astype(jnp.int32)
    column = iota((number, AUX), 1)
    aux = jnp.where(
        column == 0,
        label_int // 32,
        jnp.where(column == 1, label_int % 32, jnp.where(column == 2, 1, 0)),
    )
    aux = aux.astype(jnp.float32).astype(jnp.bfloat16)
    wide_ref[:, width : width + AUX] = jnp.dot(
        route, aux, preferred_element_type=jnp.float32
    ).astype(jnp.bfloat16)


def encode(captions, counts, target, label, params, slots):
    position, gain_in, gain_out, query_proj, pair_proj, out_proj, head_proj, temper = params
    number, length, width = captions.shape
    inner = query_proj.shape[1]
    lead = -inner % LANES
    vmem = pl.BlockSpec()
    smem = pl.BlockSpec(memory_space=pltpu.SMEM)
    hbm = pl.BlockSpec(memory_space=pl.ANY)
    return pl.pallas_call(
        tower_kernel,
        out_shape=jax.ShapeDtypeStruct((slots, width + AUX), jnp.bfloat16),
        in_specs=[smem] + [hbm] * 11,
        out_specs=vmem,
        scratch_shapes=[
            pltpu.VMEM((1, number), jnp.int32),
            pltpu.VMEM((1, number), jnp.int32),
            pltpu.VMEM((1, number), jnp.int32),
            pltpu.VMEM((number, length, width), jnp.bfloat16),
            pltpu.VMEM((length, width), jnp.bfloat16),
            pltpu.VMEM((1, width), jnp.float32),
            pltpu.VMEM((1, width), jnp.float32),
            pltpu.VMEM((inner, width), jnp.bfloat16),
            pltpu.VMEM((width, width), jnp.bfloat16),
            pltpu.VMEM((lead + inner, width), jnp.bfloat16),
            pltpu.VMEM((width, width), jnp.bfloat16),
            pltpu.VMEM((number * length, width), jnp.bfloat16),
            pltpu.VMEM((number * length, width), jnp.bfloat16),
            pltpu.SemaphoreType.DMA((10 + BATCHES,)),
        ],
        compiler_params=pltpu.CompilerParams(vmem_limit_bytes=56 * 1024 * 1024),
        cost_estimate=pl.CostEstimate(
            flops=2 * number * length * width * width,
            bytes_accessed=10_000_000,
            transcendentals=number * length * LANES,
        ),
        name="tower",
    )(
        temper,
        counts.reshape(1, number),
        target.reshape(1, number),
        label.reshape(1, number),
        captions,
        position,
        gain_in.reshape(1, width),
        gain_out.reshape(1, width),
        query_proj.T,
        pair_proj,
        out_proj,
        head_proj,
    )


def slope_of(logits, same, live):
    sign = jnp.where(same, 1.0, -1.0)
    return -sign / (1.0 + jnp.exp(sign * logits)) * live


def inverse_norm(values):
    values = values.astype(jnp.float32)
    return lax.rsqrt(jnp.sum(values * values, axis=-1, keepdims=True) + 1e-06)


def aux_rows(aux):
    row, column = iota((8, AUX), 0), iota((8, AUX), 1)
    pick = jnp.where(
        row == 0,
        jnp.where(column == 0, 32.0, jnp.where(column == 1, 1.0, 0.0)),
        jnp.where((row == 1) & (column == 2), 1.0, 0.0),
    ).astype(jnp.bfloat16)
    rows = lax.dot_general(pick, aux, NT, preferred_element_type=jnp.float32)
    return rows[0:1], rows[1:2]


def text_kernel(scale_ref, offset_ref, wide_ref, images_hbm, grad_ref, images_ref, sems):
    total, width = images_hbm.shape
    number = wide_ref.shape[0]
    chunk = total // CHUNKS
    copies = [
        pltpu.make_async_copy(
            images_hbm.at[pl.ds(part * chunk, chunk)],
            images_ref.at[pl.ds(part * chunk, chunk)],
            sems.at[part],
        )
        for part in range(CHUNKS)
    ]
    for copy in copies:
        copy.start()
    scale = scale_ref[0]
    offset = offset_ref[0]
    text = wide_ref[:, 0:width]
    label, live = aux_rows(wide_ref[:, width:])
    grad = jnp.zeros((number, width), jnp.float32)
    for part in range(CHUNKS):
        copies[part].wait()
        images = images_ref[part * chunk : (part + 1) * chunk, :]
        inverse = inverse_norm(images)
        logits = lax.dot_general(images, text, NT, preferred_element_type=jnp.float32)
        logits = (scale * inverse) * logits + offset
        index = (part * chunk + iota((chunk, 1), 0)).astype(jnp.float32)
        slopes = (slope_of(logits, label == index, live) * inverse).astype(jnp.bfloat16)
        grad = grad + lax.dot_general(slopes, images, TN, preferred_element_type=jnp.float32)
    grad_ref[...] = scale * grad


def image_kernel(scale_ref, offset_ref, start_ref, images_ref, *rest):
    number, width = images_ref.shape
    wide_refs, grad_ref = rest[:-1], rest[-1]
    images = images_ref[...]
    scale = scale_ref[0]
    offset = offset_ref[0]
    inverse = scale * inverse_norm(images)
    index = (start_ref[0] + iota((number, 1), 0)).astype(jnp.float32)
    grad = jnp.zeros((number, width), jnp.float32)
    for wide_ref in wide_refs:
        text = wide_ref[:, 0:width]
        label, live = aux_rows(wide_ref[:, width:])
        logits = lax.dot_general(images, text, NT, preferred_element_type=jnp.float32)
        slopes = slope_of(inverse * logits + offset, label == index, live).astype(jnp.bfloat16)
        grad = grad + jnp.dot(slopes, text, preferred_element_type=jnp.float32)
    grad_ref[...] = scale * grad


def text_gradient(wide, image_all, scale, offset):
    total, width = image_all.shape
    number = wide.shape[0]
    smem = pl.BlockSpec(memory_space=pltpu.SMEM)
    vmem = pl.BlockSpec(memory_space=pltpu.VMEM)
    return pl.pallas_call(
        text_kernel,
        out_shape=jax.ShapeDtypeStruct((number, width), jnp.float32),
        in_specs=[smem, smem, vmem, pl.BlockSpec(memory_space=pl.ANY)],
        out_specs=vmem,
        scratch_shapes=[
            pltpu.VMEM((total, width), jnp.bfloat16),
            pltpu.SemaphoreType.DMA((CHUNKS,)),
        ],
        compiler_params=pltpu.CompilerParams(vmem_limit_bytes=56 * 1024 * 1024),
        cost_estimate=pl.CostEstimate(
            flops=4 * total * number * width,
            bytes_accessed=2 * total * width,
            transcendentals=total * number,
        ),
        name="text_gradient",
    )(scale, offset, wide, image_all)


def image_gradient(images, wides, start, scale, offset):
    number, width = images.shape
    texts = sum(wide.shape[0] for wide in wides)
    smem = pl.BlockSpec(memory_space=pltpu.SMEM)
    vmem = pl.BlockSpec(memory_space=pltpu.VMEM)
    return pl.pallas_call(
        image_kernel,
        out_shape=jax.ShapeDtypeStruct((number, width), jnp.float32),
        in_specs=[smem, smem, smem, vmem] + [vmem] * len(wides),
        out_specs=vmem,
        compiler_params=pltpu.CompilerParams(vmem_limit_bytes=24 * 1024 * 1024),
        cost_estimate=pl.CostEstimate(
            flops=4 * texts * number * width,
            bytes_accessed=2 * texts * width,
            transcendentals=texts * number,
        ),
        name="image_gradient",
    )(scale, offset, start, images, *wides)


def loss_grads(wide, images, image_all, scale, offset):
    blocks = lax.axis_size("blk")
    zs = blocks // (XS * CS)
    count = images.shape[0]
    place = lambda z, x, c: (z * XS + x) * CS + c
    lines = [[place(z, x, c) for z in range(zs)] for x in range(XS) for c in range(CS)]
    rings = [[place(z, x, c) for x in range(XS)] for z in range(zs) for c in range(CS)]
    swap = [(place(z, x, c), place(z, x, 1 - c)) for z in range(zs) for x in range(XS) for c in range(CS)]
    first = lax.all_gather(wide, "blk", axis=0, tiled=True, axis_index_groups=lines)
    rows = first.shape[0] // 2
    firsts = [
        lax.all_gather(part, "blk", axis=0, tiled=True, axis_index_groups=rings)
        for part in (first[:rows], first[rows:])
    ]
    seconds = [lax.ppermute(part, "blk", swap) for part in firsts]
    text_sum = text_gradient(wide, image_all, scale, offset)
    start = (lax.axis_index("blk") * count).reshape(1)
    image_sum = image_gradient(images, firsts + seconds, start, scale, offset)
    return text_sum, image_sum


def local(
    captions,
    lengths,
    destination,
    labels,
    images,
    position,
    gain_in,
    gain_out,
    query_proj,
    pair_proj,
    out_proj,
    head_proj,
    temper,
    logit_scale,
    logit_bias,
):
    slots = lax.axis_size("dp")
    params = (position, gain_in, gain_out, query_proj, pair_proj, out_proj, head_proj, temper)
    own = images[0, 0]
    image_all = lax.all_gather(own, "blk", axis=0, tiled=True)
    sent = encode(captions[0, 0], lengths[0, 0], destination[0, 0], labels[0, 0], params, slots)
    wide = lax.all_to_all(sent, "dp", split_axis=0, concat_axis=0, tiled=True)
    text_sum, image_sum = loss_grads(wide, own, image_all, logit_scale, logit_bias)
    return text_sum[None, None], image_sum[None, None]


def solution(mesh):
    return jax.shard_map(
        local,
        mesh=mesh,
        in_specs=(
            P("dp", "blk", None, None, None),
            P("dp", "blk", None),
            P("dp", "blk", None),
            P("dp", "blk", None),
            P("dp", "blk", None, None),
            P(),
            P(),
            P(),
            P(),
            P(),
            P(),
            P(),
            P(),
            P(),
            P(),
        ),
        out_specs=(P("dp", "blk", None, None), P("dp", "blk", None, None)),
        check_vma=False,
    )
```

```python
import jax
import jax.numpy as jnp
from jax import lax
from jax.experimental import pallas as pl
from jax.experimental.pallas import tpu as pltpu
from jax.sharding import PartitionSpec as P

CS = 2
XS = 4
LANES = 128
AUX = 128
BATCHES = 8
CHUNKS = 4
NT = (((1,), (1,)), ((), ()))
TN = (((0,), (0,)), ((), ()))


def layer_norm(values, gain):
    center = values - jnp.mean(values, axis=-1, keepdims=True)
    spread = jnp.mean(center * center, axis=-1, keepdims=True)
    return center * lax.rsqrt(spread + 1e-06) * gain


def unit_rows(values):
    return values * lax.rsqrt(jnp.sum(values * values, axis=-1, keepdims=True) + 1e-06)


def split_dot(values, right, dims=(((1,), (0,)), ((), ()))):
    high = values.astype(jnp.bfloat16)
    low = (values - high.astype(jnp.float32)).astype(jnp.bfloat16)
    return lax.dot_general(high, right, dims, preferred_element_type=jnp.float32) + lax.dot_general(
        low, right, dims, preferred_element_type=jnp.float32
    )


def as_half(mask):
    return jnp.where(mask, 1.0, 0.0).astype(jnp.bfloat16)


def iota(shape, dimension):
    return lax.broadcasted_iota(jnp.int32, shape, dimension)


def tower_kernel(
    temper_ref,
    count_hbm,
    target_hbm,
    label_hbm,
    caption_hbm,
    position_hbm,
    gain_in_hbm,
    gain_out_hbm,
    query_hbm,
    pair_hbm,
    out_hbm,
    head_hbm,
    wide_ref,
    count_ref,
    target_ref,
    label_ref,
    caption_ref,
    position_ref,
    gain_in_ref,
    gain_out_ref,
    query_ref,
    pair_ref,
    out_ref,
    head_ref,
    normed_ref,
    kv_ref,
    sems,
):
    number, length, width = caption_ref.shape
    tokens = number * length
    inner = query_hbm.shape[0]
    heads = temper_ref.shape[0]
    size = inner // heads
    lead = out_ref.shape[0] - inner
    slots = wide_ref.shape[0]
    pair_copy = pltpu.make_async_copy(pair_hbm, pair_ref, sems.at[0])
    query_copy = pltpu.make_async_copy(query_hbm, query_ref, sems.at[1])
    out_copy = pltpu.make_async_copy(out_hbm, out_ref.at[pl.ds(lead, inner), :], sems.at[2])
    head_copy = pltpu.make_async_copy(head_hbm, head_ref, sems.at[3])
    group = number // BATCHES
    position_copy = pltpu.make_async_copy(position_hbm, position_ref, sems.at[4])
    gain_in_copy = pltpu.make_async_copy(gain_in_hbm, gain_in_ref, sems.at[5])
    gain_out_copy = pltpu.make_async_copy(gain_out_hbm, gain_out_ref, sems.at[6])
    count_copy = pltpu.make_async_copy(count_hbm, count_ref, sems.at[7])
    target_copy = pltpu.make_async_copy(target_hbm, target_ref, sems.at[8])
    label_copy = pltpu.make_async_copy(label_hbm, label_ref, sems.at[9])
    caption_copies = [
        pltpu.make_async_copy(
            caption_hbm.at[pl.ds(batch * group, group)],
            caption_ref.at[pl.ds(batch * group, group)],
            sems.at[10 + batch],
        )
        for batch in range(BATCHES)
    ]
    position_copy.start()
    gain_in_copy.start()
    for copy in caption_copies:
        copy.start()
    pair_copy.start()
    count_copy.start()
    label_copy.start()
    query_copy.start()
    out_copy.start()
    target_copy.start()
    gain_out_copy.start()
    head_copy.start()
    out_ref[0:lead, :] = jnp.zeros((lead, width), jnp.bfloat16)

    position_copy.wait()
    gain_in_copy.wait()
    gain_in = gain_in_ref[...].reshape(1, width)
    position = position_ref[...].astype(jnp.float32)
    for batch in range(BATCHES):
        start = batch * group
        caption_copies[batch].wait()
        summed = caption_ref[start : start + group].astype(jnp.float32) + position[None]
        normed = layer_norm(summed, gain_in[None]).astype(jnp.bfloat16)
        normed_ref[start * length : (start + group) * length, :] = normed.reshape(
            group * length, width
        )

    count_copy.wait()
    label_copy.wait()
    count_row = jnp.maximum(count_ref[...], 1).astype(jnp.float32)
    label_row = label_ref[...].astype(jnp.float32)
    diagonal = iota((number, number), 0) == iota((number, number), 1)
    count_col = jnp.sum(jnp.where(diagonal, count_row, 0.0), axis=1, keepdims=True)
    label_col = jnp.sum(jnp.where(diagonal, label_row, 0.0), axis=1, keepdims=True)
    last_col = count_col.astype(jnp.int32) - 1
    pick = as_half(iota((number, tokens), 1) == iota((number, tokens), 0) * length + last_col)
    pick_position = as_half(iota((number, length), 1) == last_col)
    member = as_half(iota((number, tokens), 1) // length == iota((number, tokens), 0))
    owner = iota((tokens, number), 0) // length == iota((tokens, number), 1)
    spread = as_half(owner)
    count_tok = jnp.sum(jnp.where(owner, count_row, 0.0), axis=1, keepdims=True)
    place_tok = (iota((tokens, 1), 0) % length).astype(jnp.float32)
    first = iota((inner, LANES), 1) * size
    key_heads = as_half((iota((inner, LANES), 0) >= first) & (iota((inner, LANES), 0) < first + size))
    wide_inner = lead + inner
    first = iota((LANES, wide_inner), 0) * size + lead
    value_heads = as_half(
        (iota((LANES, wide_inner), 1) >= first) & (iota((LANES, wide_inner), 1) < first + size)
    )
    lane = iota((1, LANES), 1)
    temper = jnp.zeros((1, LANES), jnp.float32)
    for head in range(heads):
        temper = jnp.where(lane == head, temper_ref[head], temper)

    pair_copy.wait()
    step = width // 3
    for start in range(0, width, step):
        kv_ref[:, start : start + step] = jnp.dot(
            normed_ref[...], pair_ref[:, start : start + step], preferred_element_type=jnp.float32
        ).astype(jnp.bfloat16)
    normed_last = jnp.dot(pick, normed_ref[...], preferred_element_type=jnp.float32).astype(
        jnp.bfloat16
    )
    flat = caption_ref[...].reshape(tokens, width)
    summed_last = jnp.dot(pick, flat, preferred_element_type=jnp.float32) + jnp.dot(
        pick_position, position_ref[...], preferred_element_type=jnp.float32
    )
    query_copy.wait()
    queries = lax.dot_general(
        normed_last, query_ref[...], NT, preferred_element_type=jnp.float32
    )
    query_norm = temper * lax.rsqrt(split_dot(queries * queries, key_heads) + 1e-06)
    query_high = queries.astype(jnp.bfloat16)
    query_low = (queries - query_high.astype(jnp.float32)).astype(jnp.bfloat16)
    norm_high = query_norm.astype(jnp.bfloat16)
    norm_low = (query_norm - norm_high.astype(jnp.float32)).astype(jnp.bfloat16)

    attended = jnp.zeros((number, wide_inner), jnp.float32)
    parts = 2
    some = tokens // parts
    for part in range(parts):
        rows = slice(part * some, (part + 1) * some)
        spread_part = spread[rows]
        query_tok = jnp.dot(
            spread_part, query_high, preferred_element_type=jnp.float32
        ) + jnp.dot(spread_part, query_low, preferred_element_type=jnp.float32)
        norm_tok = jnp.dot(
            spread_part, norm_high, preferred_element_type=jnp.float32
        ) + jnp.dot(spread_part, norm_low, preferred_element_type=jnp.float32)
        keys = kv_ref[rows, 0:inner].astype(jnp.float32)
        products = split_dot(keys * query_tok, key_heads)
        key_square = split_dot(keys * keys, key_heads)
        scores = products * lax.rsqrt(key_square + 1e-06) * norm_tok
        raised = jnp.where(place_tok[rows] < count_tok[rows], jnp.exp(scores), 0.0)
        raised = raised.reshape(some // length, length, LANES)
        probs = raised / jnp.sum(raised, axis=1, keepdims=True)
        probs = probs.reshape(some, LANES).astype(jnp.bfloat16)
        probs_wide = jnp.dot(probs, value_heads, preferred_element_type=jnp.float32)
        values = kv_ref[rows, width - wide_inner : width].astype(jnp.float32)
        weighed = probs_wide * values
        high = weighed.astype(jnp.bfloat16)
        low = (weighed - high.astype(jnp.float32)).astype(jnp.bfloat16)
        attended = (
            attended
            + jnp.dot(member[:, rows], high, preferred_element_type=jnp.float32)
            + jnp.dot(member[:, rows], low, preferred_element_type=jnp.float32)
        )
    out_copy.wait()
    residual = summed_last + jnp.dot(
        attended.astype(jnp.bfloat16), out_ref[...], preferred_element_type=jnp.float32
    )
    gain_out_copy.wait()
    final = layer_norm(residual, gain_out_ref[...].reshape(1, width)).astype(jnp.bfloat16)
    head_copy.wait()
    pooled = unit_rows(jnp.dot(final, head_ref[...], preferred_element_type=jnp.float32)).astype(
        jnp.bfloat16
    )
    target_copy.wait()
    route = as_half(target_ref[...] == iota((slots, number), 0))
    wide_ref[:, 0:width] = jnp.dot(route, pooled, preferred_element_type=jnp.float32).astype(
        jnp.bfloat16
    )
    label_int = label_col.astype(jnp.int32)
    column = iota((number, AUX), 1)
    aux = jnp.where(
        column == 0,
        label_int // 32,
        jnp.where(column == 1, label_int % 32, jnp.where(column == 2, 1, 0)),
    )
    aux = aux.astype(jnp.float32).astype(jnp.bfloat16)
    wide_ref[:, width : width + AUX] = jnp.dot(
        route, aux, preferred_element_type=jnp.float32
    ).astype(jnp.bfloat16)


def encode(captions, counts, target, label, params, slots):
    position, gain_in, gain_out, query_proj, pair_proj, out_proj, head_proj, temper = params
    number, length, width = captions.shape
    inner = query_proj.shape[1]
    lead = -inner % LANES
    vmem = pl.BlockSpec()
    smem = pl.BlockSpec(memory_space=pltpu.SMEM)
    hbm = pl.BlockSpec(memory_space=pl.ANY)
    return pl.pallas_call(
        tower_kernel,
        out_shape=jax.ShapeDtypeStruct((slots, width + AUX), jnp.bfloat16),
        in_specs=[smem] + [hbm] * 11,
        out_specs=vmem,
        scratch_shapes=[
            pltpu.VMEM((1, number), jnp.int32),
            pltpu.VMEM((1, number), jnp.int32),
            pltpu.VMEM((1, number), jnp.int32),
            pltpu.VMEM((number, length, width), jnp.bfloat16),
            pltpu.VMEM((length, width), jnp.bfloat16),
            pltpu.VMEM((width,), jnp.float32),
            pltpu.VMEM((width,), jnp.float32),
            pltpu.VMEM((inner, width), jnp.bfloat16),
            pltpu.VMEM((width, width), jnp.bfloat16),
            pltpu.VMEM((lead + inner, width), jnp.bfloat16),
            pltpu.VMEM((width, width), jnp.bfloat16),
            pltpu.VMEM((number * length, width), jnp.bfloat16),
            pltpu.VMEM((number * length, width), jnp.bfloat16),
            pltpu.SemaphoreType.DMA((10 + BATCHES,)),
        ],
        compiler_params=pltpu.CompilerParams(vmem_limit_bytes=56 * 1024 * 1024),
        cost_estimate=pl.CostEstimate(
            flops=2 * number * length * width * width,
            bytes_accessed=10_000_000,
            transcendentals=number * length * LANES,
        ),
        name="tower",
    )(
        temper,
        counts.reshape(1, number),
        target.reshape(1, number),
        label.reshape(1, number),
        captions,
        position,
        gain_in,
        gain_out,
        query_proj.T,
        pair_proj,
        out_proj,
        head_proj,
    )


def slope_of(logits, same, live):
    sign = jnp.where(same, 1.0, -1.0)
    return -sign / (1.0 + jnp.exp(sign * logits)) * live


def inverse_norm(values):
    values = values.astype(jnp.float32)
    return lax.rsqrt(jnp.sum(values * values, axis=-1, keepdims=True) + 1e-06)


def aux_rows(aux):
    row, column = iota((8, AUX), 0), iota((8, AUX), 1)
    pick = jnp.where(
        row == 0,
        jnp.where(column == 0, 32.0, jnp.where(column == 1, 1.0, 0.0)),
        jnp.where((row == 1) & (column == 2), 1.0, 0.0),
    ).astype(jnp.bfloat16)
    rows = lax.dot_general(pick, aux, NT, preferred_element_type=jnp.float32)
    return rows[0:1], rows[1:2]


def text_kernel(scale_ref, offset_ref, wide_ref, images_hbm, grad_ref, images_ref, sems):
    total, width = images_hbm.shape
    number = wide_ref.shape[0]
    chunk = total // CHUNKS
    copies = [
        pltpu.make_async_copy(
            images_hbm.at[pl.ds(part * chunk, chunk)],
            images_ref.at[pl.ds(part * chunk, chunk)],
            sems.at[part],
        )
        for part in range(CHUNKS)
    ]
    for copy in copies:
        copy.start()
    scale = scale_ref[0]
    offset = offset_ref[0]
    text = wide_ref[:, 0:width]
    label, live = aux_rows(wide_ref[:, width:])
    grad = jnp.zeros((number, width), jnp.float32)
    for part in range(CHUNKS):
        copies[part].wait()
        images = images_ref[part * chunk : (part + 1) * chunk, :]
        inverse = inverse_norm(images)
        logits = lax.dot_general(images, text, NT, preferred_element_type=jnp.float32)
        logits = (scale * inverse) * logits + offset
        index = (part * chunk + iota((chunk, 1), 0)).astype(jnp.float32)
        slopes = (slope_of(logits, label == index, live) * inverse).astype(jnp.bfloat16)
        grad = grad + lax.dot_general(slopes, images, TN, preferred_element_type=jnp.float32)
    grad_ref[...] = scale * grad


def image_kernel(scale_ref, offset_ref, start_ref, images_ref, *rest):
    number, width = images_ref.shape
    wide_refs, grad_ref = rest[:-1], rest[-1]
    images = images_ref[...]
    scale = scale_ref[0]
    offset = offset_ref[0]
    inverse = scale * inverse_norm(images)
    index = (start_ref[0] + iota((number, 1), 0)).astype(jnp.float32)
    grad = jnp.zeros((number, width), jnp.float32)
    for wide_ref in wide_refs:
        text = wide_ref[:, 0:width]
        label, live = aux_rows(wide_ref[:, width:])
        logits = lax.dot_general(images, text, NT, preferred_element_type=jnp.float32)
        slopes = slope_of(inverse * logits + offset, label == index, live).astype(jnp.bfloat16)
        grad = grad + jnp.dot(slopes, text, preferred_element_type=jnp.float32)
    grad_ref[...] = scale * grad


def text_gradient(wide, image_all, scale, offset):
    total, width = image_all.shape
    number = wide.shape[0]
    smem = pl.BlockSpec(memory_space=pltpu.SMEM)
    vmem = pl.BlockSpec(memory_space=pltpu.VMEM)
    return pl.pallas_call(
        text_kernel,
        out_shape=jax.ShapeDtypeStruct((number, width), jnp.float32),
        in_specs=[smem, smem, vmem, pl.BlockSpec(memory_space=pl.ANY)],
        out_specs=vmem,
        scratch_shapes=[
            pltpu.VMEM((total, width), jnp.bfloat16),
            pltpu.SemaphoreType.DMA((CHUNKS,)),
        ],
        compiler_params=pltpu.CompilerParams(vmem_limit_bytes=56 * 1024 * 1024),
        cost_estimate=pl.CostEstimate(
            flops=4 * total * number * width,
            bytes_accessed=2 * total * width,
            transcendentals=total * number,
        ),
        name="text_gradient",
    )(scale, offset, wide, image_all)


def image_gradient(images, wides, start, scale, offset):
    number, width = images.shape
    texts = sum(wide.shape[0] for wide in wides)
    smem = pl.BlockSpec(memory_space=pltpu.SMEM)
    vmem = pl.BlockSpec(memory_space=pltpu.VMEM)
    return pl.pallas_call(
        image_kernel,
        out_shape=jax.ShapeDtypeStruct((number, width), jnp.float32),
        in_specs=[smem, smem, smem, vmem] + [vmem] * len(wides),
        out_specs=vmem,
        compiler_params=pltpu.CompilerParams(vmem_limit_bytes=24 * 1024 * 1024),
        cost_estimate=pl.CostEstimate(
            flops=4 * texts * number * width,
            bytes_accessed=2 * texts * width,
            transcendentals=texts * number,
        ),
        name="image_gradient",
    )(scale, offset, start, images, *wides)


def spread_to(rows, groups):
    members = len(groups[0])
    blocks = jnp.broadcast_to(rows[None], (members,) + rows.shape)
    got = lax.all_to_all(
        blocks, "blk", split_axis=0, concat_axis=0, tiled=True, axis_index_groups=groups
    )
    return got.reshape(members * rows.shape[0], rows.shape[1])


def loss_grads(wide, images, image_all, scale, offset):
    blocks = lax.axis_size("blk")
    zs = blocks // (XS * CS)
    count = images.shape[0]
    place = lambda z, x, c: (z * XS + x) * CS + c
    lines = [[place(z, x, c) for z in range(zs)] for x in range(XS) for c in range(CS)]
    rings = [[place(z, x, c) for x in range(XS)] for z in range(zs) for c in range(CS)]
    swap = [
        (place(z, x, c), place(z, x, 1 - c)) for z in range(zs) for x in range(XS) for c in range(CS)
    ]
    start = (lax.axis_index("blk") * count).reshape(1)
    first = spread_to(spread_to(wide, lines), rings)
    second = lax.ppermute(first, "blk", swap)
    text_sum = text_gradient(wide, image_all, scale, offset)
    second, text_sum = lax.optimization_barrier((second, text_sum))
    image_sum = image_gradient(images, [first, second], start, scale, offset)
    return text_sum, image_sum


def local(
    captions,
    lengths,
    destination,
    labels,
    images,
    position,
    gain_in,
    gain_out,
    query_proj,
    pair_proj,
    out_proj,
    head_proj,
    temper,
    logit_scale,
    logit_bias,
):
    slots = lax.axis_size("dp")
    params = (position, gain_in, gain_out, query_proj, pair_proj, out_proj, head_proj, temper)
    own = images[0, 0]
    image_all = lax.all_gather(own, "blk", axis=0, tiled=True)
    sent = encode(captions[0, 0], lengths[0, 0], destination[0, 0], labels[0, 0], params, slots)
    halves = sent.reshape(slots, 2, sent.shape[1] // 2)
    wide = lax.all_to_all(halves, "dp", split_axis=0, concat_axis=0, tiled=True)
    wide = wide.reshape(sent.shape)
    text_sum, image_sum = loss_grads(wide, own, image_all, logit_scale, logit_bias)
    return text_sum[None, None], image_sum[None, None]


def solution(mesh):
    return jax.shard_map(
        local,
        mesh=mesh,
        in_specs=(
            P("dp", "blk", None, None, None),
            P("dp", "blk", None),
            P("dp", "blk", None),
            P("dp", "blk", None),
            P("dp", "blk", None, None),
            P(),
            P(),
            P(),
            P(),
            P(),
            P(),
            P(),
            P(),
            P(),
            P(),
        ),
        out_specs=(P("dp", "blk", None, None), P("dp", "blk", None, None)),
        check_vma=False,
    )
```

```python
import jax
import jax.numpy as jnp
from jax import lax
from jax.experimental import pallas as pl
from jax.experimental.pallas import tpu as pltpu
from jax.sharding import PartitionSpec as P

CS = 2
XS = 4
LANES = 128
AUX = 128
BATCHES = 8
NT = (((1,), (1,)), ((), ()))
TN = (((0,), (0,)), ((), ()))


def layer_norm(values, gain):
    center = values - jnp.mean(values, axis=-1, keepdims=True)
    spread = jnp.mean(center * center, axis=-1, keepdims=True)
    return center * lax.rsqrt(spread + 1e-06) * gain


def unit_rows(values):
    return values * lax.rsqrt(jnp.sum(values * values, axis=-1, keepdims=True) + 1e-06)


def split_dot(values, right, dims=(((1,), (0,)), ((), ()))):
    high = values.astype(jnp.bfloat16)
    low = (values - high.astype(jnp.float32)).astype(jnp.bfloat16)
    return lax.dot_general(high, right, dims, preferred_element_type=jnp.float32) + lax.dot_general(
        low, right, dims, preferred_element_type=jnp.float32
    )


def as_half(mask):
    return jnp.where(mask, 1.0, 0.0).astype(jnp.bfloat16)


def iota(shape, dimension):
    return lax.broadcasted_iota(jnp.int32, shape, dimension)


def tower_kernel(
    temper_ref,
    count_hbm,
    target_hbm,
    label_hbm,
    caption_hbm,
    position_hbm,
    gain_in_hbm,
    gain_out_hbm,
    query_hbm,
    pair_hbm,
    out_hbm,
    head_hbm,
    wide_ref,
    count_ref,
    target_ref,
    label_ref,
    caption_ref,
    position_ref,
    gain_in_ref,
    gain_out_ref,
    query_ref,
    pair_ref,
    out_ref,
    head_ref,
    normed_ref,
    kv_ref,
    sems,
):
    number, length, width = caption_ref.shape
    tokens = number * length
    inner = query_hbm.shape[0]
    heads = temper_ref.shape[0]
    size = inner // heads
    lead = out_ref.shape[0] - inner
    slots = wide_ref.shape[0]
    pair_copy = pltpu.make_async_copy(pair_hbm, pair_ref, sems.at[0])
    query_copy = pltpu.make_async_copy(query_hbm, query_ref, sems.at[1])
    out_copy = pltpu.make_async_copy(out_hbm, out_ref.at[pl.ds(lead, inner), :], sems.at[2])
    head_copy = pltpu.make_async_copy(head_hbm, head_ref, sems.at[3])
    group = number // BATCHES
    position_copy = pltpu.make_async_copy(position_hbm, position_ref, sems.at[4])
    gain_in_copy = pltpu.make_async_copy(gain_in_hbm, gain_in_ref, sems.at[5])
    gain_out_copy = pltpu.make_async_copy(gain_out_hbm, gain_out_ref, sems.at[6])
    count_copy = pltpu.make_async_copy(count_hbm, count_ref, sems.at[7])
    target_copy = pltpu.make_async_copy(target_hbm, target_ref, sems.at[8])
    label_copy = pltpu.make_async_copy(label_hbm, label_ref, sems.at[9])
    caption_copies = [
        pltpu.make_async_copy(
            caption_hbm.at[pl.ds(batch * group, group)],
            caption_ref.at[pl.ds(batch * group, group)],
            sems.at[10 + batch],
        )
        for batch in range(BATCHES)
    ]
    position_copy.start()
    gain_in_copy.start()
    for copy in caption_copies:
        copy.start()
    pair_copy.start()
    count_copy.start()
    label_copy.start()
    query_copy.start()
    out_copy.start()
    target_copy.start()
    gain_out_copy.start()
    head_copy.start()
    out_ref[0:lead, :] = jnp.zeros((lead, width), jnp.bfloat16)

    position_copy.wait()
    gain_in_copy.wait()
    gain_in = gain_in_ref[...].reshape(1, width)
    position = position_ref[...].astype(jnp.float32)
    for batch in range(BATCHES):
        start = batch * group
        caption_copies[batch].wait()
        summed = caption_ref[start : start + group].astype(jnp.float32) + position[None]
        normed = layer_norm(summed, gain_in[None]).astype(jnp.bfloat16)
        normed_ref[start * length : (start + group) * length, :] = normed.reshape(
            group * length, width
        )

    count_copy.wait()
    label_copy.wait()
    count_row = jnp.maximum(count_ref[...], 1).astype(jnp.float32)
    label_row = label_ref[...].astype(jnp.float32)
    diagonal = iota((number, number), 0) == iota((number, number), 1)
    count_col = jnp.sum(jnp.where(diagonal, count_row, 0.0), axis=1, keepdims=True)
    label_col = jnp.sum(jnp.where(diagonal, label_row, 0.0), axis=1, keepdims=True)
    last_col = count_col.astype(jnp.int32) - 1
    pick = as_half(iota((number, tokens), 1) == iota((number, tokens), 0) * length + last_col)
    pick_position = as_half(iota((number, length), 1) == last_col)
    member = as_half(iota((number, tokens), 1) // length == iota((number, tokens), 0))
    owner = iota((tokens, number), 0) // length == iota((tokens, number), 1)
    spread = as_half(owner)
    count_tok = jnp.sum(jnp.where(owner, count_row, 0.0), axis=1, keepdims=True)
    place_tok = (iota((tokens, 1), 0) % length).astype(jnp.float32)
    first = iota((inner, LANES), 1) * size
    key_heads = as_half((iota((inner, LANES), 0) >= first) & (iota((inner, LANES), 0) < first + size))
    wide_inner = lead + inner
    first = iota((LANES, wide_inner), 0) * size + lead
    value_heads = as_half(
        (iota((LANES, wide_inner), 1) >= first) & (iota((LANES, wide_inner), 1) < first + size)
    )
    lane = iota((1, LANES), 1)
    temper = jnp.zeros((1, LANES), jnp.float32)
    for head in range(heads):
        temper = jnp.where(lane == head, temper_ref[head], temper)

    pair_copy.wait()
    step = width // 3
    for start in range(0, width, step):
        kv_ref[:, start : start + step] = jnp.dot(
            normed_ref[...], pair_ref[:, start : start + step], preferred_element_type=jnp.float32
        ).astype(jnp.bfloat16)
    normed_last = jnp.dot(pick, normed_ref[...], preferred_element_type=jnp.float32).astype(
        jnp.bfloat16
    )
    flat = caption_ref[...].reshape(tokens, width)
    summed_last = jnp.dot(pick, flat, preferred_element_type=jnp.float32) + jnp.dot(
        pick_position, position_ref[...], preferred_element_type=jnp.float32
    )
    query_copy.wait()
    queries = lax.dot_general(
        normed_last, query_ref[...], NT, preferred_element_type=jnp.float32
    )
    query_norm = temper * lax.rsqrt(split_dot(queries * queries, key_heads) + 1e-06)
    query_high = queries.astype(jnp.bfloat16)
    query_low = (queries - query_high.astype(jnp.float32)).astype(jnp.bfloat16)
    norm_high = query_norm.astype(jnp.bfloat16)
    norm_low = (query_norm - norm_high.astype(jnp.float32)).astype(jnp.bfloat16)

    attended = jnp.zeros((number, wide_inner), jnp.float32)
    parts = 2
    some = tokens // parts
    for part in range(parts):
        rows = slice(part * some, (part + 1) * some)
        spread_part = spread[rows]
        query_tok = jnp.dot(
            spread_part, query_high, preferred_element_type=jnp.float32
        ) + jnp.dot(spread_part, query_low, preferred_element_type=jnp.float32)
        norm_tok = jnp.dot(
            spread_part, norm_high, preferred_element_type=jnp.float32
        ) + jnp.dot(spread_part, norm_low, preferred_element_type=jnp.float32)
        keys = kv_ref[rows, 0:inner].astype(jnp.float32)
        products = split_dot(keys * query_tok, key_heads)
        key_square = split_dot(keys * keys, key_heads)
        scores = products * lax.rsqrt(key_square + 1e-06) * norm_tok
        raised = jnp.where(place_tok[rows] < count_tok[rows], jnp.exp(scores), 0.0)
        raised = raised.reshape(some // length, length, LANES)
        probs = raised / jnp.sum(raised, axis=1, keepdims=True)
        probs = probs.reshape(some, LANES).astype(jnp.bfloat16)
        probs_wide = jnp.dot(probs, value_heads, preferred_element_type=jnp.float32)
        values = kv_ref[rows, width - wide_inner : width].astype(jnp.float32)
        weighed = probs_wide * values
        high = weighed.astype(jnp.bfloat16)
        low = (weighed - high.astype(jnp.float32)).astype(jnp.bfloat16)
        attended = (
            attended
            + jnp.dot(member[:, rows], high, preferred_element_type=jnp.float32)
            + jnp.dot(member[:, rows], low, preferred_element_type=jnp.float32)
        )
    out_copy.wait()
    residual = summed_last + jnp.dot(
        attended.astype(jnp.bfloat16), out_ref[...], preferred_element_type=jnp.float32
    )
    gain_out_copy.wait()
    final = layer_norm(residual, gain_out_ref[...].reshape(1, width)).astype(jnp.bfloat16)
    head_copy.wait()
    pooled = unit_rows(jnp.dot(final, head_ref[...], preferred_element_type=jnp.float32)).astype(
        jnp.bfloat16
    )
    target_copy.wait()
    route = as_half(target_ref[...] == iota((slots, number), 0))
    wide_ref[:, 0:width] = jnp.dot(route, pooled, preferred_element_type=jnp.float32).astype(
        jnp.bfloat16
    )
    label_int = label_col.astype(jnp.int32)
    column = iota((number, AUX), 1)
    aux = jnp.where(
        column == 0,
        label_int // 32,
        jnp.where(column == 1, label_int % 32, jnp.where(column == 2, 1, 0)),
    )
    aux = aux.astype(jnp.float32).astype(jnp.bfloat16)
    wide_ref[:, width : width + AUX] = jnp.dot(
        route, aux, preferred_element_type=jnp.float32
    ).astype(jnp.bfloat16)


def encode(captions, counts, target, label, params, slots):
    position, gain_in, gain_out, query_proj, pair_proj, out_proj, head_proj, temper = params
    number, length, width = captions.shape
    inner = query_proj.shape[1]
    lead = -inner % LANES
    vmem = pl.BlockSpec()
    smem = pl.BlockSpec(memory_space=pltpu.SMEM)
    hbm = pl.BlockSpec(memory_space=pl.ANY)
    return pl.pallas_call(
        tower_kernel,
        out_shape=jax.ShapeDtypeStruct((slots, width + AUX), jnp.bfloat16),
        in_specs=[smem] + [hbm] * 11,
        out_specs=vmem,
        scratch_shapes=[
            pltpu.VMEM((1, number), jnp.int32),
            pltpu.VMEM((1, number), jnp.int32),
            pltpu.VMEM((1, number), jnp.int32),
            pltpu.VMEM((number, length, width), jnp.bfloat16),
            pltpu.VMEM((length, width), jnp.bfloat16),
            pltpu.VMEM((width,), jnp.float32),
            pltpu.VMEM((width,), jnp.float32),
            pltpu.VMEM((inner, width), jnp.bfloat16),
            pltpu.VMEM((width, width), jnp.bfloat16),
            pltpu.VMEM((lead + inner, width), jnp.bfloat16),
            pltpu.VMEM((width, width), jnp.bfloat16),
            pltpu.VMEM((number * length, width), jnp.bfloat16),
            pltpu.VMEM((number * length, width), jnp.bfloat16),
            pltpu.SemaphoreType.DMA((10 + BATCHES,)),
        ],
        compiler_params=pltpu.CompilerParams(vmem_limit_bytes=56 * 1024 * 1024),
        cost_estimate=pl.CostEstimate(
            flops=2 * number * length * width * width,
            bytes_accessed=10_000_000,
            transcendentals=number * length * LANES,
        ),
        name="tower",
    )(
        temper,
        counts.reshape(1, number),
        target.reshape(1, number),
        label.reshape(1, number),
        captions,
        position,
        gain_in,
        gain_out,
        query_proj.T,
        pair_proj,
        out_proj,
        head_proj,
    )


def slope_of(logits, same, live):
    sign = jnp.where(same, 1.0, -1.0)
    return -sign / (1.0 + jnp.exp(sign * logits)) * live


def inverse_norm(values):
    values = values.astype(jnp.float32)
    return lax.rsqrt(jnp.sum(values * values, axis=-1, keepdims=True) + 1e-06)


def aux_rows(aux):
    row, column = iota((8, AUX), 0), iota((8, AUX), 1)
    pick = jnp.where(
        row == 0,
        jnp.where(column == 0, 32.0, jnp.where(column == 1, 1.0, 0.0)),
        jnp.where((row == 1) & (column == 2), 1.0, 0.0),
    ).astype(jnp.bfloat16)
    rows = lax.dot_general(pick, aux, NT, preferred_element_type=jnp.float32)
    return rows[0:1], rows[1:2]


def text_parts_kernel(scale_ref, offset_ref, start_ref, wide_ref, images_ref, parts_ref):
    number, width = images_ref.shape
    images = images_ref[...]
    text = wide_ref[:, 0:width]
    label, live = aux_rows(wide_ref[:, width:])
    inverse = inverse_norm(images)
    logits = lax.dot_general(images, text, NT, preferred_element_type=jnp.float32)
    logits = (scale_ref[0] * inverse) * logits + offset_ref[0]
    index = (start_ref[0] + iota((number, 1), 0)).astype(jnp.float32)
    slopes = (slope_of(logits, label == index, live) * inverse).astype(jnp.bfloat16)
    parts_ref[...] = lax.dot_general(
        slopes, images, TN, preferred_element_type=jnp.float32
    ).astype(jnp.bfloat16)


def image_parts_kernel(scale_ref, offset_ref, start_ref, core_ref, wide_ref, images_ref, parts_ref):
    number, width = parts_ref.shape
    count = number // XS
    text = wide_ref[:, 0:width]
    label, live = aux_rows(wide_ref[:, width:])
    for x in range(XS):
        row = pl.multiple_of((x * CS + core_ref[0]) * count, count)
        images = images_ref[pl.ds(row, count), :]
        logits = lax.dot_general(images, text, NT, preferred_element_type=jnp.float32)
        logits = (scale_ref[0] * inverse_norm(images)) * logits + offset_ref[0]
        index = (start_ref[0] + row + iota((count, 1), 0)).astype(jnp.float32)
        slopes = slope_of(logits, label == index, live).astype(jnp.bfloat16)
        parts_ref[x * count : (x + 1) * count, :] = jnp.dot(
            slopes, text, preferred_element_type=jnp.float32
        ).astype(jnp.bfloat16)


def call_parts(kernel, scalars, wide, images, rows, name):
    number, width = images.shape
    smem = pl.BlockSpec(memory_space=pltpu.SMEM)
    vmem = pl.BlockSpec(memory_space=pltpu.VMEM)
    return pl.pallas_call(
        kernel,
        out_shape=jax.ShapeDtypeStruct((rows, width), jnp.bfloat16),
        in_specs=[smem] * len(scalars) + [vmem, vmem],
        out_specs=vmem,
        compiler_params=pltpu.CompilerParams(vmem_limit_bytes=24 * 1024 * 1024),
        cost_estimate=pl.CostEstimate(
            flops=4 * wide.shape[0] * number * width,
            bytes_accessed=4 * number * width,
            transcendentals=wide.shape[0] * number,
        ),
        name=name,
    )(*scalars, wide, images)


def exchange(blocks, groups):
    return lax.all_to_all(
        blocks, "blk", split_axis=0, concat_axis=0, tiled=True, axis_index_groups=groups
    )


def spread_to(rows, groups):
    members = len(groups[0])
    got = exchange(jnp.broadcast_to(rows[None], (members,) + rows.shape), groups)
    return got.reshape(members * rows.shape[0], rows.shape[1])


def groups_of(blocks):
    zs = blocks // (XS * CS)
    place = lambda z, x, c: (z * XS + x) * CS + c
    lines = [[place(z, x, c) for z in range(zs)] for x in range(XS) for c in range(CS)]
    rings = [[place(z, x, c) for x in range(XS)] for z in range(zs) for c in range(CS)]
    pairs = [[place(z, x, c) for c in range(CS)] for z in range(zs) for x in range(XS)]
    return lines, rings, pairs


def both_cores(rows, pairs):
    return lax.all_gather(rows, "blk", axis=0, tiled=True, axis_index_groups=pairs)


def summed_parts(got, scale):
    return scale * jnp.sum(got.astype(jnp.float32), axis=0)


def loss_grads(wide, images, scale, offset, groups):
    lines, rings, pairs = groups
    number, width = images.shape
    count = number // (XS * CS)
    slots = wide.shape[0]
    mine = lax.axis_index("blk")
    core = (mine % CS).reshape(1)
    start = (mine // (XS * CS) * number).reshape(1)
    line = spread_to(wide, lines)
    text_parts = call_parts(
        text_parts_kernel, (scale, offset, start), line, images, line.shape[0], "text_parts"
    )
    text_got = exchange(text_parts.reshape(-1, slots, width), lines)
    image_parts = call_parts(
        image_parts_kernel,
        (scale, offset, start, core),
        both_cores(line, pairs),
        images,
        XS * count,
        "image_parts",
    )
    image_got = exchange(image_parts.reshape(-1, count, width), rings)
    return summed_parts(text_got, scale), summed_parts(image_got, scale)


def local(
    captions,
    lengths,
    destination,
    labels,
    images,
    position,
    gain_in,
    gain_out,
    query_proj,
    pair_proj,
    out_proj,
    head_proj,
    temper,
    logit_scale,
    logit_bias,
):
    slots = lax.axis_size("dp")
    params = (position, gain_in, gain_out, query_proj, pair_proj, out_proj, head_proj, temper)
    groups = groups_of(lax.axis_size("blk"))
    pair = both_cores(images[0, 0], groups[2])
    rows, pair = lax.optimization_barrier((captions, pair))
    near = spread_to(pair, groups[1])
    sent = encode(rows[0, 0], lengths[0, 0], destination[0, 0], labels[0, 0], params, slots)
    sent, near = lax.optimization_barrier((sent, near))
    halves = sent.reshape(slots, 2, sent.shape[1] // 2)
    wide = lax.all_to_all(halves, "dp", split_axis=0, concat_axis=0, tiled=True)
    wide = wide.reshape(sent.shape)
    text_sum, image_sum = loss_grads(wide, near, logit_scale, logit_bias, groups)
    return text_sum[None, None], image_sum[None, None]


def solution(mesh):
    return jax.shard_map(
        local,
        mesh=mesh,
        in_specs=(
            P("dp", "blk", None, None, None),
            P("dp", "blk", None),
            P("dp", "blk", None),
            P("dp", "blk", None),
            P("dp", "blk", None, None),
            P(),
            P(),
            P(),
            P(),
            P(),
            P(),
            P(),
            P(),
            P(),
            P(),
        ),
        out_specs=(P("dp", "blk", None, None), P("dp", "blk", None, None)),
        check_vma=False,
    )
```

```python
import jax
import jax.numpy as jnp
from jax import lax
from jax.experimental import pallas as pl
from jax.experimental.pallas import tpu as pltpu
from jax.sharding import PartitionSpec as P

CS = 2
XS = 4
LANES = 128
AUX = 128
BATCHES = 8
NT = (((1,), (1,)), ((), ()))
TN = (((0,), (0,)), ((), ()))


def layer_norm(values, gain):
    center = values - jnp.mean(values, axis=-1, keepdims=True)
    spread = jnp.mean(center * center, axis=-1, keepdims=True)
    return center * lax.rsqrt(spread + 1e-06) * gain


def unit_rows(values):
    return values * lax.rsqrt(jnp.sum(values * values, axis=-1, keepdims=True) + 1e-06)


def split_dot(values, right, dims=(((1,), (0,)), ((), ()))):
    high = values.astype(jnp.bfloat16)
    low = (values - high.astype(jnp.float32)).astype(jnp.bfloat16)
    return lax.dot_general(high, right, dims, preferred_element_type=jnp.float32) + lax.dot_general(
        low, right, dims, preferred_element_type=jnp.float32
    )


def as_half(mask):
    return jnp.where(mask, 1.0, 0.0).astype(jnp.bfloat16)


def iota(shape, dimension):
    return lax.broadcasted_iota(jnp.int32, shape, dimension)


def tower_kernel(
    temper_ref,
    count_hbm,
    target_hbm,
    label_hbm,
    caption_hbm,
    position_hbm,
    gain_in_hbm,
    gain_out_hbm,
    query_hbm,
    pair_hbm,
    out_hbm,
    head_hbm,
    wide_ref,
    count_ref,
    target_ref,
    label_ref,
    caption_ref,
    position_ref,
    gain_in_ref,
    gain_out_ref,
    query_ref,
    pair_ref,
    out_ref,
    head_ref,
    normed_ref,
    kv_ref,
    sems,
):
    number, length, width = caption_ref.shape
    tokens = number * length
    inner = query_hbm.shape[0]
    heads = temper_ref.shape[0]
    size = inner // heads
    lead = out_ref.shape[0] - inner
    slots = wide_ref.shape[0]
    pair_copy = pltpu.make_async_copy(pair_hbm, pair_ref, sems.at[0])
    query_copy = pltpu.make_async_copy(query_hbm, query_ref, sems.at[1])
    out_copy = pltpu.make_async_copy(out_hbm, out_ref.at[pl.ds(lead, inner), :], sems.at[2])
    head_copy = pltpu.make_async_copy(head_hbm, head_ref, sems.at[3])
    group = number // BATCHES
    position_copy = pltpu.make_async_copy(position_hbm, position_ref, sems.at[4])
    gain_in_copy = pltpu.make_async_copy(gain_in_hbm, gain_in_ref, sems.at[5])
    gain_out_copy = pltpu.make_async_copy(gain_out_hbm, gain_out_ref, sems.at[6])
    count_copy = pltpu.make_async_copy(count_hbm, count_ref, sems.at[7])
    target_copy = pltpu.make_async_copy(target_hbm, target_ref, sems.at[8])
    label_copy = pltpu.make_async_copy(label_hbm, label_ref, sems.at[9])
    caption_copies = [
        pltpu.make_async_copy(
            caption_hbm.at[pl.ds(batch * group, group)],
            caption_ref.at[pl.ds(batch * group, group)],
            sems.at[10 + batch],
        )
        for batch in range(BATCHES)
    ]
    position_copy.start()
    gain_in_copy.start()
    for copy in caption_copies:
        copy.start()
    pair_copy.start()
    count_copy.start()
    label_copy.start()
    query_copy.start()
    out_copy.start()
    target_copy.start()
    gain_out_copy.start()
    head_copy.start()
    out_ref[0:lead, :] = jnp.zeros((lead, width), jnp.bfloat16)

    position_copy.wait()
    gain_in_copy.wait()
    gain_in = gain_in_ref[...].reshape(1, width)
    position = position_ref[...].astype(jnp.float32)
    for batch in range(BATCHES):
        start = batch * group
        caption_copies[batch].wait()
        summed = caption_ref[start : start + group].astype(jnp.float32) + position[None]
        normed = layer_norm(summed, gain_in[None]).astype(jnp.bfloat16)
        normed_ref[start * length : (start + group) * length, :] = normed.reshape(
            group * length, width
        )

    count_copy.wait()
    label_copy.wait()
    count_row = jnp.maximum(count_ref[...], 1).astype(jnp.float32)
    label_row = label_ref[...].astype(jnp.float32)
    diagonal = iota((number, number), 0) == iota((number, number), 1)
    count_col = jnp.sum(jnp.where(diagonal, count_row, 0.0), axis=1, keepdims=True)
    label_col = jnp.sum(jnp.where(diagonal, label_row, 0.0), axis=1, keepdims=True)
    last_col = count_col.astype(jnp.int32) - 1
    pick = as_half(iota((number, tokens), 1) == iota((number, tokens), 0) * length + last_col)
    pick_position = as_half(iota((number, length), 1) == last_col)
    member = as_half(iota((number, tokens), 1) // length == iota((number, tokens), 0))
    owner = iota((tokens, number), 0) // length == iota((tokens, number), 1)
    spread = as_half(owner)
    count_tok = jnp.sum(jnp.where(owner, count_row, 0.0), axis=1, keepdims=True)
    place_tok = (iota((tokens, 1), 0) % length).astype(jnp.float32)
    first = iota((inner, LANES), 1) * size
    key_heads = as_half((iota((inner, LANES), 0) >= first) & (iota((inner, LANES), 0) < first + size))
    wide_inner = lead + inner
    first = iota((LANES, wide_inner), 0) * size + lead
    value_heads = as_half(
        (iota((LANES, wide_inner), 1) >= first) & (iota((LANES, wide_inner), 1) < first + size)
    )
    lane = iota((1, LANES), 1)
    temper = jnp.zeros((1, LANES), jnp.float32)
    for head in range(heads):
        temper = jnp.where(lane == head, temper_ref[head], temper)

    pair_copy.wait()
    step = width // 3
    for start in range(0, width, step):
        kv_ref[:, start : start + step] = jnp.dot(
            normed_ref[...], pair_ref[:, start : start + step], preferred_element_type=jnp.float32
        ).astype(jnp.bfloat16)
    normed_last = jnp.dot(pick, normed_ref[...], preferred_element_type=jnp.float32).astype(
        jnp.bfloat16
    )
    flat = caption_ref[...].reshape(tokens, width)
    summed_last = jnp.dot(pick, flat, preferred_element_type=jnp.float32) + jnp.dot(
        pick_position, position_ref[...], preferred_element_type=jnp.float32
    )
    query_copy.wait()
    queries = lax.dot_general(
        normed_last, query_ref[...], NT, preferred_element_type=jnp.float32
    )
    query_norm = temper * lax.rsqrt(split_dot(queries * queries, key_heads) + 1e-06)
    query_high = queries.astype(jnp.bfloat16)
    query_low = (queries - query_high.astype(jnp.float32)).astype(jnp.bfloat16)
    norm_high = query_norm.astype(jnp.bfloat16)
    norm_low = (query_norm - norm_high.astype(jnp.float32)).astype(jnp.bfloat16)

    attended = jnp.zeros((number, wide_inner), jnp.float32)
    parts = 2
    some = tokens // parts
    for part in range(parts):
        rows = slice(part * some, (part + 1) * some)
        spread_part = spread[rows]
        query_tok = jnp.dot(
            spread_part, query_high, preferred_element_type=jnp.float32
        ) + jnp.dot(spread_part, query_low, preferred_element_type=jnp.float32)
        norm_tok = jnp.dot(
            spread_part, norm_high, preferred_element_type=jnp.float32
        ) + jnp.dot(spread_part, norm_low, preferred_element_type=jnp.float32)
        keys = kv_ref[rows, 0:inner].astype(jnp.float32)
        products = split_dot(keys * query_tok, key_heads)
        key_square = split_dot(keys * keys, key_heads)
        scores = products * lax.rsqrt(key_square + 1e-06) * norm_tok
        raised = jnp.where(place_tok[rows] < count_tok[rows], jnp.exp(scores), 0.0)
        raised = raised.reshape(some // length, length, LANES)
        probs = raised / jnp.sum(raised, axis=1, keepdims=True)
        probs = probs.reshape(some, LANES).astype(jnp.bfloat16)
        probs_wide = jnp.dot(probs, value_heads, preferred_element_type=jnp.float32)
        values = kv_ref[rows, width - wide_inner : width].astype(jnp.float32)
        weighed = probs_wide * values
        high = weighed.astype(jnp.bfloat16)
        low = (weighed - high.astype(jnp.float32)).astype(jnp.bfloat16)
        attended = (
            attended
            + jnp.dot(member[:, rows], high, preferred_element_type=jnp.float32)
            + jnp.dot(member[:, rows], low, preferred_element_type=jnp.float32)
        )
    out_copy.wait()
    residual = summed_last + jnp.dot(
        attended.astype(jnp.bfloat16), out_ref[...], preferred_element_type=jnp.float32
    )
    gain_out_copy.wait()
    final = layer_norm(residual, gain_out_ref[...].reshape(1, width)).astype(jnp.bfloat16)
    head_copy.wait()
    pooled = unit_rows(jnp.dot(final, head_ref[...], preferred_element_type=jnp.float32)).astype(
        jnp.bfloat16
    )
    target_copy.wait()
    route = as_half(target_ref[...] == iota((slots, number), 0))
    wide_ref[:, 0:width] = jnp.dot(route, pooled, preferred_element_type=jnp.float32).astype(
        jnp.bfloat16
    )
    label_int = label_col.astype(jnp.int32)
    column = iota((number, AUX), 1)
    aux = jnp.where(
        column == 0,
        label_int // 32,
        jnp.where(column == 1, label_int % 32, jnp.where(column == 2, 1, 0)),
    )
    aux = aux.astype(jnp.float32).astype(jnp.bfloat16)
    wide_ref[:, width : width + AUX] = jnp.dot(
        route, aux, preferred_element_type=jnp.float32
    ).astype(jnp.bfloat16)


def encode(captions, counts, target, label, params, slots):
    position, gain_in, gain_out, query_proj, pair_proj, out_proj, head_proj, temper = params
    number, length, width = captions.shape
    inner = query_proj.shape[1]
    lead = -inner % LANES
    vmem = pl.BlockSpec()
    smem = pl.BlockSpec(memory_space=pltpu.SMEM)
    hbm = pl.BlockSpec(memory_space=pl.ANY)
    return pl.pallas_call(
        tower_kernel,
        out_shape=jax.ShapeDtypeStruct((slots, width + AUX), jnp.bfloat16),
        in_specs=[smem] + [hbm] * 11,
        out_specs=vmem,
        scratch_shapes=[
            pltpu.VMEM((1, number), jnp.int32),
            pltpu.VMEM((1, number), jnp.int32),
            pltpu.VMEM((1, number), jnp.int32),
            pltpu.VMEM((number, length, width), jnp.bfloat16),
            pltpu.VMEM((length, width), jnp.bfloat16),
            pltpu.VMEM((width,), jnp.float32),
            pltpu.VMEM((width,), jnp.float32),
            pltpu.VMEM((inner, width), jnp.bfloat16),
            pltpu.VMEM((width, width), jnp.bfloat16),
            pltpu.VMEM((lead + inner, width), jnp.bfloat16),
            pltpu.VMEM((width, width), jnp.bfloat16),
            pltpu.VMEM((number * length, width), jnp.bfloat16),
            pltpu.VMEM((number * length, width), jnp.bfloat16),
            pltpu.SemaphoreType.DMA((10 + BATCHES,)),
        ],
        compiler_params=pltpu.CompilerParams(vmem_limit_bytes=56 * 1024 * 1024),
        cost_estimate=pl.CostEstimate(
            flops=2 * number * length * width * width,
            bytes_accessed=10_000_000,
            transcendentals=number * length * LANES,
        ),
        name="tower",
    )(
        temper,
        counts.reshape(1, number),
        target.reshape(1, number),
        label.reshape(1, number),
        captions,
        position,
        gain_in,
        gain_out,
        query_proj.T,
        pair_proj,
        out_proj,
        head_proj,
    )


def slope_of(logits, same, live):
    sign = jnp.where(same, 1.0, -1.0)
    return -sign / (1.0 + jnp.exp(sign * logits)) * live


def inverse_norm(values):
    values = values.astype(jnp.float32)
    return lax.rsqrt(jnp.sum(values * values, axis=-1, keepdims=True) + 1e-06)


def aux_rows(aux):
    row, column = iota((8, AUX), 0), iota((8, AUX), 1)
    pick = jnp.where(
        row == 0,
        jnp.where(column == 0, 32.0, jnp.where(column == 1, 1.0, 0.0)),
        jnp.where((row == 1) & (column == 2), 1.0, 0.0),
    ).astype(jnp.bfloat16)
    rows = lax.dot_general(pick, aux, NT, preferred_element_type=jnp.float32)
    return rows[0:1], rows[1:2]


def text_parts_kernel(scale_ref, offset_ref, start_ref, wide_ref, images_ref, parts_ref):
    number, width = images_ref.shape
    count = number // (XS * CS)
    images = images_ref[...]
    text = wide_ref[:, 0:width]
    label, live = aux_rows(wide_ref[:, width:])
    inverse = inverse_norm(images)
    logits = lax.dot_general(images, text, NT, preferred_element_type=jnp.float32)
    logits = (scale_ref[0] * inverse) * logits + offset_ref[0]
    row = iota((number, 1), 0)
    place = (row // count % XS) * CS + row // (count * XS)
    index = (start_ref[0] + place * count + row % count).astype(jnp.float32)
    slopes = (slope_of(logits, label == index, live) * inverse).astype(jnp.bfloat16)
    parts_ref[...] = lax.dot_general(
        slopes, images, TN, preferred_element_type=jnp.float32
    ).astype(jnp.bfloat16)


def image_parts_kernel(scale_ref, offset_ref, start_ref, core_ref, wide_ref, images_ref, parts_ref):
    number, width = images_ref.shape
    count = number // XS
    images = images_ref[...]
    text = wide_ref[:, 0:width]
    label, live = aux_rows(wide_ref[:, width:])
    logits = lax.dot_general(images, text, NT, preferred_element_type=jnp.float32)
    logits = (scale_ref[0] * inverse_norm(images)) * logits + offset_ref[0]
    row = iota((number, 1), 0)
    place = row // count * CS + core_ref[0]
    index = (start_ref[0] + place * count + row % count).astype(jnp.float32)
    slopes = slope_of(logits, label == index, live).astype(jnp.bfloat16)
    parts_ref[...] = jnp.dot(slopes, text, preferred_element_type=jnp.float32).astype(jnp.bfloat16)


def call_parts(kernel, scalars, wide, images, rows, name):
    number, width = images.shape
    smem = pl.BlockSpec(memory_space=pltpu.SMEM)
    vmem = pl.BlockSpec(memory_space=pltpu.VMEM)
    return pl.pallas_call(
        kernel,
        out_shape=jax.ShapeDtypeStruct((rows, width), jnp.bfloat16),
        in_specs=[smem] * len(scalars) + [vmem, vmem],
        out_specs=vmem,
        compiler_params=pltpu.CompilerParams(vmem_limit_bytes=24 * 1024 * 1024),
        cost_estimate=pl.CostEstimate(
            flops=4 * wide.shape[0] * number * width,
            bytes_accessed=4 * number * width,
            transcendentals=wide.shape[0] * number,
        ),
        name=name,
    )(*scalars, wide, images)


def exchange(blocks, groups):
    return lax.all_to_all(
        blocks, "blk", split_axis=0, concat_axis=0, tiled=True, axis_index_groups=groups
    )


def spread_to(rows, groups):
    members = len(groups[0])
    got = exchange(jnp.broadcast_to(rows[None], (members,) + rows.shape), groups)
    return got.reshape(members * rows.shape[0], rows.shape[1])


def groups_of(blocks):
    zs = blocks // (XS * CS)
    place = lambda z, x, c: (z * XS + x) * CS + c
    lines = [[place(z, x, c) for z in range(zs)] for x in range(XS) for c in range(CS)]
    rings = [[place(z, x, c) for x in range(XS)] for z in range(zs) for c in range(CS)]
    pairs = [[place(z, x, c) for c in range(CS)] for z in range(zs) for x in range(XS)]
    return lines, rings, pairs


def both_cores(rows, pairs):
    return lax.all_gather(rows, "blk", axis=0, tiled=True, axis_index_groups=pairs)


def summed_parts(got, scale):
    return scale * jnp.sum(got.astype(jnp.float32), axis=0)


def loss_grads(wide, near, scale, offset, groups):
    lines, rings, pairs = groups
    number, width = near.shape
    count = number // XS
    slots = wide.shape[0]
    mine = lax.axis_index("blk")
    core = (mine % CS).reshape(1)
    start = (mine // (XS * CS) * (number * CS)).reshape(1)
    line = spread_to(wide, lines)
    text_parts = call_parts(
        text_parts_kernel,
        (scale, offset, start),
        line,
        both_cores(near, pairs),
        line.shape[0],
        "text_parts",
    )
    text_parts, line = lax.optimization_barrier((text_parts, line))
    text_got = exchange(text_parts.reshape(-1, slots, width), lines)
    image_parts = call_parts(
        image_parts_kernel,
        (scale, offset, start, core),
        both_cores(line, pairs),
        near,
        number,
        "image_parts",
    )
    text_got, image_parts = lax.optimization_barrier((text_got, image_parts))
    image_got = exchange(image_parts.reshape(-1, count, width), rings)
    return summed_parts(text_got, scale), summed_parts(image_got, scale)


def local(
    captions,
    lengths,
    destination,
    labels,
    images,
    position,
    gain_in,
    gain_out,
    query_proj,
    pair_proj,
    out_proj,
    head_proj,
    temper,
    logit_scale,
    logit_bias,
):
    slots = lax.axis_size("dp")
    params = (position, gain_in, gain_out, query_proj, pair_proj, out_proj, head_proj, temper)
    groups = groups_of(lax.axis_size("blk"))
    near = spread_to(images[0, 0], groups[1])
    sent = encode(captions[0, 0], lengths[0, 0], destination[0, 0], labels[0, 0], params, slots)
    sent, near = lax.optimization_barrier((sent, near))
    halves = sent.reshape(slots, 2, sent.shape[1] // 2)
    wide = lax.all_to_all(halves, "dp", split_axis=0, concat_axis=0, tiled=True)
    wide, near = lax.optimization_barrier((wide, near))
    wide = wide.reshape(sent.shape)
    text_sum, image_sum = loss_grads(wide, near, logit_scale, logit_bias, groups)
    return text_sum[None, None], image_sum[None, None]


def solution(mesh):
    return jax.shard_map(
        local,
        mesh=mesh,
        in_specs=(
            P("dp", "blk", None, None, None),
            P("dp", "blk", None),
            P("dp", "blk", None),
            P("dp", "blk", None),
            P("dp", "blk", None, None),
            P(),
            P(),
            P(),
            P(),
            P(),
            P(),
            P(),
            P(),
            P(),
            P(),
        ),
        out_specs=(P("dp", "blk", None, None), P("dp", "blk", None, None)),
        check_vma=False,
    )
```

```python
import jax
import jax.numpy as jnp
from jax import lax
from jax.experimental import pallas as pl
from jax.experimental.pallas import tpu as pltpu
from jax.sharding import PartitionSpec as P

CS = 2
XS = 4
ZS = 4
LANES = 128
AUX = 128
BATCHES = 2
NT = (((1,), (1,)), ((), ()))
TN = (((0,), (0,)), ((), ()))


def layer_norm(values, gain):
    center = values - jnp.mean(values, axis=-1, keepdims=True)
    spread = jnp.mean(center * center, axis=-1, keepdims=True)
    return center * lax.rsqrt(spread + 1e-06) * gain


def unit_rows(values):
    return values * lax.rsqrt(jnp.sum(values * values, axis=-1, keepdims=True) + 1e-06)


def split_dot(values, right, dims=(((1,), (0,)), ((), ()))):
    high = values.astype(jnp.bfloat16)
    low = (values - high.astype(jnp.float32)).astype(jnp.bfloat16)
    return lax.dot_general(high, right, dims, preferred_element_type=jnp.float32) + lax.dot_general(
        low, right, dims, preferred_element_type=jnp.float32
    )


def as_half(mask):
    return jnp.where(mask, 1.0, 0.0).astype(jnp.bfloat16)


def iota(shape, dimension):
    return lax.broadcasted_iota(jnp.int32, shape, dimension)


def tower_kernel(
    temper_ref,
    count_hbm,
    target_hbm,
    label_hbm,
    caption_hbm,
    position_hbm,
    gain_in_hbm,
    gain_out_hbm,
    query_hbm,
    pair_hbm,
    out_hbm,
    head_hbm,
    wide_ref,
    count_ref,
    target_ref,
    label_ref,
    caption_ref,
    position_ref,
    gain_in_ref,
    gain_out_ref,
    query_ref,
    pair_ref,
    out_ref,
    head_ref,
    normed_ref,
    kv_ref,
    sems,
):
    number, length, width = caption_ref.shape
    tokens = number * length
    inner = query_hbm.shape[0]
    heads = temper_ref.shape[0]
    size = inner // heads
    lead = out_ref.shape[0] - inner
    slots = wide_ref.shape[0]
    pair_copy = pltpu.make_async_copy(pair_hbm, pair_ref, sems.at[0])
    query_copy = pltpu.make_async_copy(query_hbm, query_ref, sems.at[1])
    out_copy = pltpu.make_async_copy(out_hbm, out_ref.at[pl.ds(lead, inner), :], sems.at[2])
    head_copy = pltpu.make_async_copy(head_hbm, head_ref, sems.at[3])
    group = number // BATCHES
    position_copy = pltpu.make_async_copy(position_hbm, position_ref, sems.at[4])
    gain_in_copy = pltpu.make_async_copy(gain_in_hbm, gain_in_ref, sems.at[5])
    gain_out_copy = pltpu.make_async_copy(gain_out_hbm, gain_out_ref, sems.at[6])
    count_copy = pltpu.make_async_copy(count_hbm, count_ref, sems.at[7])
    target_copy = pltpu.make_async_copy(target_hbm, target_ref, sems.at[8])
    label_copy = pltpu.make_async_copy(label_hbm, label_ref, sems.at[9])
    caption_copies = [
        pltpu.make_async_copy(
            caption_hbm.at[pl.ds(batch * group, group)],
            caption_ref.at[pl.ds(batch * group, group)],
            sems.at[10 + batch],
        )
        for batch in range(BATCHES)
    ]
    position_copy.start()
    gain_in_copy.start()
    for copy in caption_copies:
        copy.start()
    pair_copy.start()
    count_copy.start()
    label_copy.start()
    query_copy.start()
    out_copy.start()
    target_copy.start()
    gain_out_copy.start()
    head_copy.start()
    out_ref[0:lead, :] = jnp.zeros((lead, width), jnp.bfloat16)

    position_copy.wait()
    gain_in_copy.wait()
    gain_in = gain_in_ref[...].reshape(1, width)
    position = position_ref[...].astype(jnp.float32)
    for batch in range(BATCHES):
        start = batch * group
        caption_copies[batch].wait()
        summed = caption_ref[start : start + group].astype(jnp.float32) + position[None]
        normed = layer_norm(summed, gain_in[None]).astype(jnp.bfloat16)
        normed_ref[start * length : (start + group) * length, :] = normed.reshape(
            group * length, width
        )

    count_copy.wait()
    label_copy.wait()
    count_row = jnp.maximum(count_ref[...], 1).astype(jnp.float32)
    label_row = label_ref[...].astype(jnp.float32)
    diagonal = iota((number, number), 0) == iota((number, number), 1)
    count_col = jnp.sum(jnp.where(diagonal, count_row, 0.0), axis=1, keepdims=True)
    label_col = jnp.sum(jnp.where(diagonal, label_row, 0.0), axis=1, keepdims=True)
    last_col = count_col.astype(jnp.int32) - 1
    pick = as_half(iota((number, tokens), 1) == iota((number, tokens), 0) * length + last_col)
    pick_position = as_half(iota((number, length), 1) == last_col)
    member = as_half(iota((number, tokens), 1) // length == iota((number, tokens), 0))
    owner = iota((tokens, number), 0) // length == iota((tokens, number), 1)
    spread = as_half(owner)
    count_tok = jnp.sum(jnp.where(owner, count_row, 0.0), axis=1, keepdims=True)
    place_tok = (iota((tokens, 1), 0) % length).astype(jnp.float32)
    first = iota((inner, LANES), 1) * size
    key_heads = as_half((iota((inner, LANES), 0) >= first) & (iota((inner, LANES), 0) < first + size))
    wide_inner = lead + inner
    first = iota((LANES, wide_inner), 0) * size + lead
    value_heads = as_half(
        (iota((LANES, wide_inner), 1) >= first) & (iota((LANES, wide_inner), 1) < first + size)
    )
    lane = iota((1, LANES), 1)
    temper = jnp.zeros((1, LANES), jnp.float32)
    for head in range(heads):
        temper = jnp.where(lane == head, temper_ref[head], temper)

    pair_copy.wait()
    step = width
    for start in range(0, width, step):
        kv_ref[:, start : start + step] = jnp.dot(
            normed_ref[...], pair_ref[:, start : start + step], preferred_element_type=jnp.float32
        ).astype(jnp.bfloat16)
    normed_last = jnp.dot(pick, normed_ref[...], preferred_element_type=jnp.float32).astype(
        jnp.bfloat16
    )
    flat = caption_ref[...].reshape(tokens, width)
    summed_last = jnp.dot(pick, flat, preferred_element_type=jnp.float32) + jnp.dot(
        pick_position, position_ref[...], preferred_element_type=jnp.float32
    )
    query_copy.wait()
    queries = lax.dot_general(
        normed_last, query_ref[...], NT, preferred_element_type=jnp.float32
    )
    query_norm = temper * lax.rsqrt(split_dot(queries * queries, key_heads) + 1e-06)
    query_high = queries.astype(jnp.bfloat16)
    query_low = (queries - query_high.astype(jnp.float32)).astype(jnp.bfloat16)
    norm_high = query_norm.astype(jnp.bfloat16)
    norm_low = (query_norm - norm_high.astype(jnp.float32)).astype(jnp.bfloat16)

    attended = jnp.zeros((number, wide_inner), jnp.float32)
    parts = 1
    some = tokens // parts
    for part in range(parts):
        rows = slice(part * some, (part + 1) * some)
        spread_part = spread[rows]
        query_tok = jnp.dot(
            spread_part, query_high, preferred_element_type=jnp.float32
        ) + jnp.dot(spread_part, query_low, preferred_element_type=jnp.float32)
        norm_tok = jnp.dot(
            spread_part, norm_high, preferred_element_type=jnp.float32
        ) + jnp.dot(spread_part, norm_low, preferred_element_type=jnp.float32)
        keys = kv_ref[rows, 0:inner].astype(jnp.float32)
        products = split_dot(keys * query_tok, key_heads)
        key_square = split_dot(keys * keys, key_heads)
        scores = products * lax.rsqrt(key_square + 1e-06) * norm_tok
        raised = jnp.where(place_tok[rows] < count_tok[rows], jnp.exp(scores), 0.0)
        raised = raised.reshape(some // length, length, LANES)
        probs = raised / jnp.sum(raised, axis=1, keepdims=True)
        probs = probs.reshape(some, LANES).astype(jnp.bfloat16)
        probs_wide = jnp.dot(probs, value_heads, preferred_element_type=jnp.float32)
        values = kv_ref[rows, width - wide_inner : width].astype(jnp.float32)
        weighed = probs_wide * values
        high = weighed.astype(jnp.bfloat16)
        low = (weighed - high.astype(jnp.float32)).astype(jnp.bfloat16)
        attended = (
            attended
            + jnp.dot(member[:, rows], high, preferred_element_type=jnp.float32)
            + jnp.dot(member[:, rows], low, preferred_element_type=jnp.float32)
        )
    out_copy.wait()
    residual = summed_last + jnp.dot(
        attended.astype(jnp.bfloat16), out_ref[...], preferred_element_type=jnp.float32
    )
    gain_out_copy.wait()
    final = layer_norm(residual, gain_out_ref[...].reshape(1, width)).astype(jnp.bfloat16)
    head_copy.wait()
    pooled = unit_rows(jnp.dot(final, head_ref[...], preferred_element_type=jnp.float32)).astype(
        jnp.bfloat16
    )
    target_copy.wait()
    route = as_half(target_ref[...] == iota((slots, number), 0))
    wide_ref[:, 0:width] = jnp.dot(route, pooled, preferred_element_type=jnp.float32).astype(
        jnp.bfloat16
    )
    label_int = label_col.astype(jnp.int32)
    column = iota((number, AUX), 1)
    aux = jnp.where(
        column == 0,
        label_int // 32,
        jnp.where(column == 1, label_int % 32, jnp.where(column == 2, 1, 0)),
    )
    aux = aux.astype(jnp.float32).astype(jnp.bfloat16)
    wide_ref[:, width : width + AUX] = jnp.dot(
        route, aux, preferred_element_type=jnp.float32
    ).astype(jnp.bfloat16)


def encode(captions, counts, target, label, params, slots):
    position, gain_in, gain_out, query_proj, pair_proj, out_proj, head_proj, temper = params
    number, length, width = captions.shape
    inner = query_proj.shape[1]
    lead = -inner % LANES
    vmem = pl.BlockSpec()
    smem = pl.BlockSpec(memory_space=pltpu.SMEM)
    hbm = pl.BlockSpec(memory_space=pl.ANY)
    return pl.pallas_call(
        tower_kernel,
        out_shape=jax.ShapeDtypeStruct((slots, width + AUX), jnp.bfloat16),
        in_specs=[smem] + [hbm] * 11,
        out_specs=vmem,
        scratch_shapes=[
            pltpu.VMEM((1, number), jnp.int32),
            pltpu.VMEM((1, number), jnp.int32),
            pltpu.VMEM((1, number), jnp.int32),
            pltpu.VMEM((number, length, width), jnp.bfloat16),
            pltpu.VMEM((length, width), jnp.bfloat16),
            pltpu.VMEM((width,), jnp.float32),
            pltpu.VMEM((width,), jnp.float32),
            pltpu.VMEM((inner, width), jnp.bfloat16),
            pltpu.VMEM((width, width), jnp.bfloat16),
            pltpu.VMEM((lead + inner, width), jnp.bfloat16),
            pltpu.VMEM((width, width), jnp.bfloat16),
            pltpu.VMEM((number * length, width), jnp.bfloat16),
            pltpu.VMEM((number * length, width), jnp.bfloat16),
            pltpu.SemaphoreType.DMA((10 + BATCHES,)),
        ],
        compiler_params=pltpu.CompilerParams(vmem_limit_bytes=56 * 1024 * 1024),
        cost_estimate=pl.CostEstimate(
            flops=2 * number * length * width * width,
            bytes_accessed=10_000_000,
            transcendentals=number * length * LANES,
        ),
        name="tower",
    )(
        temper,
        counts.reshape(1, number),
        target.reshape(1, number),
        label.reshape(1, number),
        captions,
        position,
        gain_in,
        gain_out,
        query_proj.T,
        pair_proj,
        out_proj,
        head_proj,
    )


def slope_of(logits, same, live):
    sign = jnp.where(same, 1.0, -1.0)
    return -sign / (1.0 + jnp.exp(sign * logits)) * live


def inverse_norm(values):
    values = values.astype(jnp.float32)
    return lax.rsqrt(jnp.sum(values * values, axis=-1, keepdims=True) + 1e-06)


def aux_rows(aux):
    row, column = iota((8, AUX), 0), iota((8, AUX), 1)
    pick = jnp.where(
        row == 0,
        jnp.where(column == 0, 32.0, jnp.where(column == 1, 1.0, 0.0)),
        jnp.where((row == 1) & (column == 2), 1.0, 0.0),
    ).astype(jnp.bfloat16)
    rows = lax.dot_general(pick, aux, NT, preferred_element_type=jnp.float32)
    return rows[0:1], rows[1:2]


def text_parts_kernel(scale_ref, offset_ref, start_ref, wide_ref, images_ref, parts_ref):
    number, width = images_ref.shape
    count = number // (ZS * CS)
    images = images_ref[...]
    text = wide_ref[:, 0:width]
    label, live = aux_rows(wide_ref[:, width:])
    inverse = inverse_norm(images)
    logits = lax.dot_general(images, text, NT, preferred_element_type=jnp.float32)
    logits = (scale_ref[0] * inverse) * logits + offset_ref[0]
    row = iota((number, 1), 0)
    place = (row // count % ZS) * (XS * CS) + row // (count * ZS)
    index = (start_ref[0] + place * count + row % count).astype(jnp.float32)
    slopes = (slope_of(logits, label == index, live) * inverse).astype(jnp.bfloat16)
    parts_ref[...] = lax.dot_general(
        slopes, images, TN, preferred_element_type=jnp.float32
    ).astype(jnp.bfloat16)


def image_parts_kernel(scale_ref, offset_ref, start_ref, core_ref, wide_ref, images_ref, parts_ref):
    number, width = images_ref.shape
    count = number // ZS
    images = images_ref[...]
    text = wide_ref[:, 0:width]
    label, live = aux_rows(wide_ref[:, width:])
    logits = lax.dot_general(images, text, NT, preferred_element_type=jnp.float32)
    logits = (scale_ref[0] * inverse_norm(images)) * logits + offset_ref[0]
    row = iota((number, 1), 0)
    place = row // count * (XS * CS) + core_ref[0]
    index = (start_ref[0] + place * count + row % count).astype(jnp.float32)
    slopes = slope_of(logits, label == index, live).astype(jnp.bfloat16)
    parts_ref[...] = jnp.dot(slopes, text, preferred_element_type=jnp.float32).astype(jnp.bfloat16)


def call_parts(kernel, scalars, wide, images, rows, name):
    number, width = images.shape
    smem = pl.BlockSpec(memory_space=pltpu.SMEM)
    vmem = pl.BlockSpec(memory_space=pltpu.VMEM)
    return pl.pallas_call(
        kernel,
        out_shape=jax.ShapeDtypeStruct((rows, width), jnp.bfloat16),
        in_specs=[smem] * len(scalars) + [vmem, vmem],
        out_specs=vmem,
        compiler_params=pltpu.CompilerParams(vmem_limit_bytes=24 * 1024 * 1024),
        cost_estimate=pl.CostEstimate(
            flops=4 * wide.shape[0] * number * width,
            bytes_accessed=4 * number * width,
            transcendentals=wide.shape[0] * number,
        ),
        name=name,
    )(*scalars, wide, images)


def exchange(blocks, groups):
    return lax.all_to_all(
        blocks, "blk", split_axis=0, concat_axis=0, tiled=True, axis_index_groups=groups
    )


def spread_to(rows, groups):
    members = len(groups[0])
    got = exchange(jnp.broadcast_to(rows[None], (members,) + rows.shape), groups)
    return got.reshape(members * rows.shape[0], rows.shape[1])


def groups_of():
    place = lambda z, x, c: (z * XS + x) * CS + c
    lines = [[place(z, x, c) for z in range(ZS)] for x in range(XS) for c in range(CS)]
    rings = [[place(z, x, c) for x in range(XS)] for z in range(ZS) for c in range(CS)]
    pairs = [[place(z, x, c) for c in range(CS)] for z in range(ZS) for x in range(XS)]
    return lines, rings, pairs


def both_cores(rows, pairs):
    return lax.all_gather(rows, "blk", axis=0, tiled=True, axis_index_groups=pairs)


def summed_parts(got, scale):
    return scale * jnp.sum(got.astype(jnp.float32), axis=0)


def loss_grads(wide, near, scale, offset, groups):
    lines, rings, pairs = groups
    number, width = near.shape
    count = number // ZS
    slots = wide.shape[0]
    mine = lax.axis_index("blk")
    core = (mine % CS).reshape(1)
    start = (mine // CS % XS * (CS * count)).reshape(1)
    ring = spread_to(wide, rings)
    text_parts = call_parts(
        text_parts_kernel,
        (scale, offset, start),
        ring,
        both_cores(near, pairs),
        ring.shape[0],
        "text_parts",
    )
    text_parts, ring = lax.optimization_barrier((text_parts, ring))
    text_got = exchange(text_parts.reshape(-1, slots, width), rings)
    image_parts = call_parts(
        image_parts_kernel,
        (scale, offset, start, core),
        both_cores(ring, pairs),
        near,
        number,
        "image_parts",
    )
    text_got, image_parts = lax.optimization_barrier((text_got, image_parts))
    image_got = exchange(image_parts.reshape(-1, count, width), lines)
    return summed_parts(text_got, scale), summed_parts(image_got, scale)


def local(
    captions,
    lengths,
    destination,
    labels,
    images,
    position,
    gain_in,
    gain_out,
    query_proj,
    pair_proj,
    out_proj,
    head_proj,
    temper,
    logit_scale,
    logit_bias,
):
    slots = lax.axis_size("dp")
    params = (position, gain_in, gain_out, query_proj, pair_proj, out_proj, head_proj, temper)
    groups = groups_of()
    near = spread_to(images[0, 0], groups[0])
    sent = encode(captions[0, 0], lengths[0, 0], destination[0, 0], labels[0, 0], params, slots)
    sent, near = lax.optimization_barrier((sent, near))
    halves = sent.reshape(slots, 2, sent.shape[1] // 2)
    wide = lax.all_to_all(halves, "dp", split_axis=0, concat_axis=0, tiled=True)
    wide, near = lax.optimization_barrier((wide, near))
    wide = wide.reshape(sent.shape)
    text_sum, image_sum = loss_grads(wide, near, logit_scale, logit_bias, groups)
    return text_sum[None, None], image_sum[None, None]


def solution(mesh):
    return jax.shard_map(
        local,
        mesh=mesh,
        in_specs=(
            P("dp", "blk", None, None, None),
            P("dp", "blk", None),
            P("dp", "blk", None),
            P("dp", "blk", None),
            P("dp", "blk", None, None),
            P(),
            P(),
            P(),
            P(),
            P(),
            P(),
            P(),
            P(),
            P(),
            P(),
        ),
        out_specs=(P("dp", "blk", None, None), P("dp", "blk", None, None)),
        check_vma=False,
    )
```

```python
import jax
import jax.numpy as jnp
from jax import lax
from jax.experimental import pallas as pl
from jax.experimental.pallas import tpu as pltpu
from jax.sharding import PartitionSpec as P

CS = 2
XS = 4
ZS = 4
LANES = 128
AUX = 128
BATCHES = 2
NT = (((1,), (1,)), ((), ()))
TN = (((0,), (0,)), ((), ()))


def layer_norm(values, gain):
    center = values - jnp.mean(values, axis=-1, keepdims=True)
    spread = jnp.mean(center * center, axis=-1, keepdims=True)
    return center * lax.rsqrt(spread + 1e-06) * gain


def unit_rows(values):
    return values * lax.rsqrt(jnp.sum(values * values, axis=-1, keepdims=True) + 1e-06)


def split_dot(values, right, dims=(((1,), (0,)), ((), ()))):
    high = values.astype(jnp.bfloat16)
    low = (values - high.astype(jnp.float32)).astype(jnp.bfloat16)
    return lax.dot_general(high, right, dims, preferred_element_type=jnp.float32) + lax.dot_general(
        low, right, dims, preferred_element_type=jnp.float32
    )


def as_half(mask):
    return jnp.where(mask, 1.0, 0.0).astype(jnp.bfloat16)


def iota(shape, dimension):
    return lax.broadcasted_iota(jnp.int32, shape, dimension)


def tower_kernel(
    temper_ref,
    count_hbm,
    target_hbm,
    label_hbm,
    caption_hbm,
    position_hbm,
    gain_in_hbm,
    gain_out_hbm,
    query_hbm,
    pair_hbm,
    out_hbm,
    head_hbm,
    wide_ref,
    count_ref,
    target_ref,
    label_ref,
    caption_ref,
    position_ref,
    gain_in_ref,
    gain_out_ref,
    query_ref,
    pair_ref,
    out_ref,
    head_ref,
    normed_ref,
    kv_ref,
    sems,
):
    number, length, width = caption_ref.shape
    tokens = number * length
    inner = query_hbm.shape[0]
    heads = temper_ref.shape[0]
    size = inner // heads
    lead = out_ref.shape[0] - inner
    slots = wide_ref.shape[0]
    pair_copy = pltpu.make_async_copy(pair_hbm, pair_ref, sems.at[0])
    query_copy = pltpu.make_async_copy(query_hbm, query_ref, sems.at[1])
    out_copy = pltpu.make_async_copy(out_hbm, out_ref.at[pl.ds(lead, inner), :], sems.at[2])
    head_copy = pltpu.make_async_copy(head_hbm, head_ref, sems.at[3])
    group = number // BATCHES
    position_copy = pltpu.make_async_copy(position_hbm, position_ref, sems.at[4])
    gain_in_copy = pltpu.make_async_copy(gain_in_hbm, gain_in_ref, sems.at[5])
    gain_out_copy = pltpu.make_async_copy(gain_out_hbm, gain_out_ref, sems.at[6])
    count_copy = pltpu.make_async_copy(count_hbm, count_ref, sems.at[7])
    target_copy = pltpu.make_async_copy(target_hbm, target_ref, sems.at[8])
    label_copy = pltpu.make_async_copy(label_hbm, label_ref, sems.at[9])
    caption_copies = [
        pltpu.make_async_copy(
            caption_hbm.at[pl.ds(batch * group, group)],
            caption_ref.at[pl.ds(batch * group, group)],
            sems.at[10 + batch],
        )
        for batch in range(BATCHES)
    ]
    position_copy.start()
    gain_in_copy.start()
    for copy in caption_copies:
        copy.start()
    pair_copy.start()
    count_copy.start()
    label_copy.start()
    query_copy.start()
    out_copy.start()
    target_copy.start()
    gain_out_copy.start()
    head_copy.start()
    out_ref[0:lead, :] = jnp.zeros((lead, width), jnp.bfloat16)

    position_copy.wait()
    gain_in_copy.wait()
    gain_in = gain_in_ref[...].reshape(1, width)
    position = position_ref[...].astype(jnp.float32)
    for batch in range(BATCHES):
        start = batch * group
        caption_copies[batch].wait()
        summed = caption_ref[start : start + group].astype(jnp.float32) + position[None]
        normed = layer_norm(summed, gain_in[None]).astype(jnp.bfloat16)
        normed_ref[start * length : (start + group) * length, :] = normed.reshape(
            group * length, width
        )

    count_copy.wait()
    label_copy.wait()
    count_row = jnp.maximum(count_ref[...], 1).astype(jnp.float32)
    label_row = label_ref[...].astype(jnp.float32)
    diagonal = iota((number, number), 0) == iota((number, number), 1)
    count_col = jnp.sum(jnp.where(diagonal, count_row, 0.0), axis=1, keepdims=True)
    label_col = jnp.sum(jnp.where(diagonal, label_row, 0.0), axis=1, keepdims=True)
    last_col = count_col.astype(jnp.int32) - 1
    pick = as_half(iota((number, tokens), 1) == iota((number, tokens), 0) * length + last_col)
    pick_position = as_half(iota((number, length), 1) == last_col)
    member = as_half(iota((number, tokens), 1) // length == iota((number, tokens), 0))
    owner = iota((tokens, number), 0) // length == iota((tokens, number), 1)
    spread = as_half(owner)
    count_tok = jnp.sum(jnp.where(owner, count_row, 0.0), axis=1, keepdims=True)
    place_tok = (iota((tokens, 1), 0) % length).astype(jnp.float32)
    first = iota((inner, LANES), 1) * size
    key_heads = as_half((iota((inner, LANES), 0) >= first) & (iota((inner, LANES), 0) < first + size))
    wide_inner = lead + inner
    first = iota((LANES, wide_inner), 0) * size + lead
    value_heads = as_half(
        (iota((LANES, wide_inner), 1) >= first) & (iota((LANES, wide_inner), 1) < first + size)
    )
    lane = iota((1, LANES), 1)
    temper = jnp.zeros((1, LANES), jnp.float32)
    for head in range(heads):
        temper = jnp.where(lane == head, temper_ref[head], temper)

    pair_copy.wait()
    step = width
    for start in range(0, width, step):
        kv_ref[:, start : start + step] = jnp.dot(
            normed_ref[...], pair_ref[:, start : start + step], preferred_element_type=jnp.float32
        ).astype(jnp.bfloat16)
    normed_last = jnp.dot(pick, normed_ref[...], preferred_element_type=jnp.float32).astype(
        jnp.bfloat16
    )
    flat = caption_ref[...].reshape(tokens, width)
    summed_last = jnp.dot(pick, flat, preferred_element_type=jnp.float32) + jnp.dot(
        pick_position, position_ref[...], preferred_element_type=jnp.float32
    )
    query_copy.wait()
    queries = lax.dot_general(
        normed_last, query_ref[...], NT, preferred_element_type=jnp.float32
    )
    query_norm = temper * lax.rsqrt(split_dot(queries * queries, key_heads) + 1e-06)
    query_high = queries.astype(jnp.bfloat16)
    query_low = (queries - query_high.astype(jnp.float32)).astype(jnp.bfloat16)
    norm_high = query_norm.astype(jnp.bfloat16)
    norm_low = (query_norm - norm_high.astype(jnp.float32)).astype(jnp.bfloat16)

    attended = jnp.zeros((number, wide_inner), jnp.float32)
    parts = 1
    some = tokens // parts
    for part in range(parts):
        rows = slice(part * some, (part + 1) * some)
        spread_part = spread[rows]
        query_tok = jnp.dot(
            spread_part, query_high, preferred_element_type=jnp.float32
        ) + jnp.dot(spread_part, query_low, preferred_element_type=jnp.float32)
        norm_tok = jnp.dot(
            spread_part, norm_high, preferred_element_type=jnp.float32
        ) + jnp.dot(spread_part, norm_low, preferred_element_type=jnp.float32)
        keys = kv_ref[rows, 0:inner].astype(jnp.float32)
        products = split_dot(keys * query_tok, key_heads)
        key_square = split_dot(keys * keys, key_heads)
        scores = products * lax.rsqrt(key_square + 1e-06) * norm_tok
        raised = jnp.where(place_tok[rows] < count_tok[rows], jnp.exp(scores), 0.0)
        raised = raised.reshape(some // length, length, LANES)
        probs = raised / jnp.sum(raised, axis=1, keepdims=True)
        probs = probs.reshape(some, LANES).astype(jnp.bfloat16)
        probs_wide = jnp.dot(probs, value_heads, preferred_element_type=jnp.float32)
        values = kv_ref[rows, width - wide_inner : width].astype(jnp.float32)
        weighed = probs_wide * values
        high = weighed.astype(jnp.bfloat16)
        low = (weighed - high.astype(jnp.float32)).astype(jnp.bfloat16)
        attended = (
            attended
            + jnp.dot(member[:, rows], high, preferred_element_type=jnp.float32)
            + jnp.dot(member[:, rows], low, preferred_element_type=jnp.float32)
        )
    out_copy.wait()
    residual = summed_last + jnp.dot(
        attended.astype(jnp.bfloat16), out_ref[...], preferred_element_type=jnp.float32
    )
    gain_out_copy.wait()
    final = layer_norm(residual, gain_out_ref[...].reshape(1, width)).astype(jnp.bfloat16)
    head_copy.wait()
    pooled = unit_rows(jnp.dot(final, head_ref[...], preferred_element_type=jnp.float32)).astype(
        jnp.bfloat16
    )
    target_copy.wait()
    route = as_half(target_ref[...] == iota((slots, number), 0))
    wide_ref[:, 0:width] = jnp.dot(route, pooled, preferred_element_type=jnp.float32).astype(
        jnp.bfloat16
    )
    label_int = label_col.astype(jnp.int32)
    column = iota((number, AUX), 1)
    aux = jnp.where(
        column == 0,
        label_int // 32,
        jnp.where(column == 1, label_int % 32, jnp.where(column == 2, 1, 0)),
    )
    aux = aux.astype(jnp.float32).astype(jnp.bfloat16)
    wide_ref[:, width : width + AUX] = jnp.dot(
        route, aux, preferred_element_type=jnp.float32
    ).astype(jnp.bfloat16)


def encode(captions, counts, target, label, params, slots):
    position, gain_in, gain_out, query_proj, pair_proj, out_proj, head_proj, temper = params
    number, length, width = captions.shape
    inner = query_proj.shape[1]
    lead = -inner % LANES
    vmem = pl.BlockSpec()
    smem = pl.BlockSpec(memory_space=pltpu.SMEM)
    hbm = pl.BlockSpec(memory_space=pl.ANY)
    return pl.pallas_call(
        tower_kernel,
        out_shape=jax.ShapeDtypeStruct((slots, width + AUX), jnp.bfloat16),
        in_specs=[smem] + [hbm] * 11,
        out_specs=vmem,
        scratch_shapes=[
            pltpu.VMEM((1, number), jnp.int32),
            pltpu.VMEM((1, number), jnp.int32),
            pltpu.VMEM((1, number), jnp.int32),
            pltpu.VMEM((number, length, width), jnp.bfloat16),
            pltpu.VMEM((length, width), jnp.bfloat16),
            pltpu.VMEM((width,), jnp.float32),
            pltpu.VMEM((width,), jnp.float32),
            pltpu.VMEM((inner, width), jnp.bfloat16),
            pltpu.VMEM((width, width), jnp.bfloat16),
            pltpu.VMEM((lead + inner, width), jnp.bfloat16),
            pltpu.VMEM((width, width), jnp.bfloat16),
            pltpu.VMEM((number * length, width), jnp.bfloat16),
            pltpu.VMEM((number * length, width), jnp.bfloat16),
            pltpu.SemaphoreType.DMA((10 + BATCHES,)),
        ],
        compiler_params=pltpu.CompilerParams(vmem_limit_bytes=56 * 1024 * 1024),
        cost_estimate=pl.CostEstimate(
            flops=2 * number * length * width * width,
            bytes_accessed=10_000_000,
            transcendentals=number * length * LANES,
        ),
        name="tower",
    )(
        temper,
        counts.reshape(1, number),
        target.reshape(1, number),
        label.reshape(1, number),
        captions,
        position,
        gain_in,
        gain_out,
        query_proj.T,
        pair_proj,
        out_proj,
        head_proj,
    )


def slope_of(logits, same, live):
    sign = jnp.where(same, 1.0, -1.0)
    return -sign / (1.0 + jnp.exp(sign * logits)) * live


def inverse_norm(values):
    values = values.astype(jnp.float32)
    return lax.rsqrt(jnp.sum(values * values, axis=-1, keepdims=True) + 1e-06)


def aux_rows(aux):
    row, column = iota((8, AUX), 0), iota((8, AUX), 1)
    pick = jnp.where(
        row == 0,
        jnp.where(column == 0, 32.0, jnp.where(column == 1, 1.0, 0.0)),
        jnp.where((row == 1) & (column == 2), 1.0, 0.0),
    ).astype(jnp.bfloat16)
    rows = lax.dot_general(pick, aux, NT, preferred_element_type=jnp.float32)
    return rows[0:1], rows[1:2]


def places(mine_ref):
    mine = mine_ref[0]
    return mine // (XS * CS), mine // CS % XS, mine % CS


def text_parts_kernel(scale_ref, offset_ref, mine_ref, wide_ref, images_ref, parts_ref):
    number, width = images_ref.shape
    count = number // (ZS * CS)
    z, x, _ = places(mine_ref)
    images = images_ref[...]
    text = wide_ref[:, 0:width]
    label, live = aux_rows(wide_ref[:, width:])
    inverse = inverse_norm(images)
    logits = lax.dot_general(images, text, NT, preferred_element_type=jnp.float32)
    logits = (scale_ref[0] * inverse) * logits + offset_ref[0]
    row = iota((number, 1), 0)
    place = (((row // count % ZS) ^ z) * XS + x) * CS + row // (count * ZS)
    index = (place * count + row % count).astype(jnp.float32)
    slopes = (slope_of(logits, label == index, live) * inverse).astype(jnp.bfloat16)
    parts_ref[...] = lax.dot_general(
        slopes, images, TN, preferred_element_type=jnp.float32
    ).astype(jnp.bfloat16)


def image_parts_kernel(scale_ref, offset_ref, mine_ref, wide_ref, images_ref, parts_ref):
    number, width = images_ref.shape
    count = number // ZS
    z, x, core = places(mine_ref)
    images = images_ref[...]
    text = wide_ref[:, 0:width]
    label, live = aux_rows(wide_ref[:, width:])
    logits = lax.dot_general(images, text, NT, preferred_element_type=jnp.float32)
    logits = (scale_ref[0] * inverse_norm(images)) * logits + offset_ref[0]
    row = iota((number, 1), 0)
    place = ((row // count ^ z) * XS + x) * CS + core
    index = (place * count + row % count).astype(jnp.float32)
    slopes = slope_of(logits, label == index, live).astype(jnp.bfloat16)
    parts = jnp.dot(slopes, text, preferred_element_type=jnp.float32).astype(jnp.bfloat16)
    for block in range(ZS):
        first = pl.multiple_of((z ^ block) * count, count)
        parts_ref[pl.ds(first, count), :] = parts[block * count : (block + 1) * count]


def call_parts(kernel, scalars, wide, images, rows, name):
    number, width = images.shape
    smem = pl.BlockSpec(memory_space=pltpu.SMEM)
    vmem = pl.BlockSpec(memory_space=pltpu.VMEM)
    return pl.pallas_call(
        kernel,
        out_shape=jax.ShapeDtypeStruct((rows, width), jnp.bfloat16),
        in_specs=[smem] * len(scalars) + [vmem, vmem],
        out_specs=vmem,
        compiler_params=pltpu.CompilerParams(vmem_limit_bytes=24 * 1024 * 1024),
        cost_estimate=pl.CostEstimate(
            flops=4 * wide.shape[0] * number * width,
            bytes_accessed=4 * number * width,
            transcendentals=wide.shape[0] * number,
        ),
        name=name,
    )(*scalars, wide, images)


def exchange(blocks, groups):
    return lax.all_to_all(
        blocks, "blk", split_axis=0, concat_axis=0, tiled=True, axis_index_groups=groups
    )


def spread_to(rows, groups):
    members = len(groups[0])
    got = exchange(jnp.broadcast_to(rows[None], (members,) + rows.shape), groups)
    return got.reshape(members * rows.shape[0], rows.shape[1])


def groups_of():
    place = lambda z, x, c: (z * XS + x) * CS + c
    lines = [[place(z, x, c) for z in range(ZS)] for x in range(XS) for c in range(CS)]
    rings = [[place(z, x, c) for x in range(XS)] for z in range(ZS) for c in range(CS)]
    pairs = [[place(z, x, c) for c in range(CS)] for z in range(ZS) for x in range(XS)]
    return lines, rings, pairs


def across(rows, bit):
    place = lambda z, x, c: (z * XS + x) * CS + c
    swap = [
        (place(z, x, c), place(z ^ bit, x, c))
        for z in range(ZS)
        for x in range(XS)
        for c in range(CS)
    ]
    return lax.ppermute(rows, "blk", swap)


def both_cores(rows, pairs):
    return lax.all_gather(rows, "blk", axis=0, tiled=True, axis_index_groups=pairs)


def summed_parts(got, scale):
    return scale * jnp.sum(got.astype(jnp.float32), axis=0)


def loss_grads(wide, near, scale, offset, groups):
    lines, rings, pairs = groups
    number, width = near.shape
    count = number // ZS
    slots = wide.shape[0]
    mine = lax.axis_index("blk").reshape(1)
    ring = spread_to(wide, rings)
    text_parts = call_parts(
        text_parts_kernel,
        (scale, offset, mine),
        ring,
        both_cores(near, pairs),
        ring.shape[0],
        "text_parts",
    )
    text_parts, ring = lax.optimization_barrier((text_parts, ring))
    text_got = exchange(text_parts.reshape(-1, slots, width), rings)
    image_parts = call_parts(
        image_parts_kernel,
        (scale, offset, mine),
        both_cores(ring, pairs),
        near,
        number,
        "image_parts",
    )
    text_got, image_parts = lax.optimization_barrier((text_got, image_parts))
    image_got = exchange(image_parts.reshape(-1, count, width), lines)
    return summed_parts(text_got, scale), summed_parts(image_got, scale)


def local(
    captions,
    lengths,
    destination,
    labels,
    images,
    position,
    gain_in,
    gain_out,
    query_proj,
    pair_proj,
    out_proj,
    head_proj,
    temper,
    logit_scale,
    logit_bias,
):
    slots = lax.axis_size("dp")
    params = (position, gain_in, gain_out, query_proj, pair_proj, out_proj, head_proj, temper)
    groups = groups_of()
    own = images[0, 0]
    beside = across(own, 1)
    sent = encode(captions[0, 0], lengths[0, 0], destination[0, 0], labels[0, 0], params, slots)
    two = jnp.concatenate([own, beside])
    sent, two = lax.optimization_barrier((sent, two))
    far = across(two, 2)
    halves = sent.reshape(slots, 2, sent.shape[1] // 2)
    wide = lax.all_to_all(halves, "dp", split_axis=0, concat_axis=0, tiled=True)
    wide, far = lax.optimization_barrier((wide, far))
    near = jnp.concatenate([two, far])
    wide = wide.reshape(sent.shape)
    text_sum, image_sum = loss_grads(wide, near, logit_scale, logit_bias, groups)
    return text_sum[None, None], image_sum[None, None]


def solution(mesh):
    return jax.shard_map(
        local,
        mesh=mesh,
        in_specs=(
            P("dp", "blk", None, None, None),
            P("dp", "blk", None),
            P("dp", "blk", None),
            P("dp", "blk", None),
            P("dp", "blk", None, None),
            P(),
            P(),
            P(),
            P(),
            P(),
            P(),
            P(),
            P(),
            P(),
            P(),
        ),
        out_specs=(P("dp", "blk", None, None), P("dp", "blk", None, None)),
        check_vma=False,
    )
```

```python
import jax
import jax.numpy as jnp
from jax import lax
from jax.experimental import pallas as pl
from jax.experimental.pallas import tpu as pltpu
from jax.sharding import PartitionSpec as P

CS = 2
XS = 4
ZS = 4
LANES = 128
AUX = 128
BATCHES = 2
NT = (((1,), (1,)), ((), ()))
TN = (((0,), (0,)), ((), ()))


def layer_norm(values, gain):
    center = values - jnp.mean(values, axis=-1, keepdims=True)
    spread = jnp.mean(center * center, axis=-1, keepdims=True)
    return center * lax.rsqrt(spread + 1e-06) * gain


def unit_rows(values):
    return values * lax.rsqrt(jnp.sum(values * values, axis=-1, keepdims=True) + 1e-06)


def split_dot(values, right, dims=(((1,), (0,)), ((), ()))):
    high = values.astype(jnp.bfloat16)
    low = (values - high.astype(jnp.float32)).astype(jnp.bfloat16)
    return lax.dot_general(high, right, dims, preferred_element_type=jnp.float32) + lax.dot_general(
        low, right, dims, preferred_element_type=jnp.float32
    )


def as_half(mask):
    return jnp.where(mask, 1.0, 0.0).astype(jnp.bfloat16)


def iota(shape, dimension):
    return lax.broadcasted_iota(jnp.int32, shape, dimension)


def tower_kernel(
    temper_ref,
    count_hbm,
    target_hbm,
    label_hbm,
    caption_hbm,
    position_hbm,
    gain_in_hbm,
    gain_out_hbm,
    query_hbm,
    pair_hbm,
    out_hbm,
    head_hbm,
    wide_ref,
    count_ref,
    target_ref,
    label_ref,
    caption_ref,
    position_ref,
    gain_in_ref,
    gain_out_ref,
    query_ref,
    pair_ref,
    out_ref,
    head_ref,
    normed_ref,
    kv_ref,
    sems,
):
    number, length, width = caption_ref.shape
    tokens = number * length
    inner = query_hbm.shape[0]
    heads = temper_ref.shape[0]
    size = inner // heads
    lead = out_ref.shape[0] - inner
    slots = wide_ref.shape[0]
    pair_copy = pltpu.make_async_copy(pair_hbm, pair_ref, sems.at[0])
    query_copy = pltpu.make_async_copy(query_hbm, query_ref, sems.at[1])
    out_copy = pltpu.make_async_copy(out_hbm, out_ref.at[pl.ds(lead, inner), :], sems.at[2])
    head_copy = pltpu.make_async_copy(head_hbm, head_ref, sems.at[3])
    group = number // BATCHES
    position_copy = pltpu.make_async_copy(position_hbm, position_ref, sems.at[4])
    gain_in_copy = pltpu.make_async_copy(gain_in_hbm, gain_in_ref, sems.at[5])
    gain_out_copy = pltpu.make_async_copy(gain_out_hbm, gain_out_ref, sems.at[6])
    count_copy = pltpu.make_async_copy(count_hbm, count_ref, sems.at[7])
    target_copy = pltpu.make_async_copy(target_hbm, target_ref, sems.at[8])
    label_copy = pltpu.make_async_copy(label_hbm, label_ref, sems.at[9])
    caption_copies = [
        pltpu.make_async_copy(
            caption_hbm.at[pl.ds(batch * group, group)],
            caption_ref.at[pl.ds(batch * group, group)],
            sems.at[10 + batch],
        )
        for batch in range(BATCHES)
    ]
    position_copy.start()
    gain_in_copy.start()
    for copy in caption_copies:
        copy.start()
    pair_copy.start()
    count_copy.start()
    label_copy.start()
    query_copy.start()
    out_copy.start()
    target_copy.start()
    gain_out_copy.start()
    head_copy.start()
    out_ref[0:lead, :] = jnp.zeros((lead, width), jnp.bfloat16)

    position_copy.wait()
    gain_in_copy.wait()
    gain_in = gain_in_ref[...].reshape(1, width)
    position = position_ref[...].astype(jnp.float32)
    for batch in range(BATCHES):
        start = batch * group
        caption_copies[batch].wait()
        summed = caption_ref[start : start + group].astype(jnp.float32) + position[None]
        normed = layer_norm(summed, gain_in[None]).astype(jnp.bfloat16)
        normed_ref[start * length : (start + group) * length, :] = normed.reshape(
            group * length, width
        )

    count_copy.wait()
    label_copy.wait()
    count_row = jnp.maximum(count_ref[...], 1).astype(jnp.float32)
    label_row = label_ref[...].astype(jnp.float32)
    diagonal = iota((number, number), 0) == iota((number, number), 1)
    count_col = jnp.sum(jnp.where(diagonal, count_row, 0.0), axis=1, keepdims=True)
    label_col = jnp.sum(jnp.where(diagonal, label_row, 0.0), axis=1, keepdims=True)
    last_col = count_col.astype(jnp.int32) - 1
    pick = as_half(iota((number, tokens), 1) == iota((number, tokens), 0) * length + last_col)
    pick_position = as_half(iota((number, length), 1) == last_col)
    member = as_half(iota((number, tokens), 1) // length == iota((number, tokens), 0))
    owner = iota((tokens, number), 0) // length == iota((tokens, number), 1)
    spread = as_half(owner)
    count_tok = jnp.sum(jnp.where(owner, count_row, 0.0), axis=1, keepdims=True)
    place_tok = (iota((tokens, 1), 0) % length).astype(jnp.float32)
    first = iota((inner, LANES), 1) * size
    key_heads = as_half((iota((inner, LANES), 0) >= first) & (iota((inner, LANES), 0) < first + size))
    wide_inner = lead + inner
    first = iota((LANES, wide_inner), 0) * size + lead
    value_heads = as_half(
        (iota((LANES, wide_inner), 1) >= first) & (iota((LANES, wide_inner), 1) < first + size)
    )
    lane = iota((1, LANES), 1)
    temper = jnp.zeros((1, LANES), jnp.float32)
    for head in range(heads):
        temper = jnp.where(lane == head, temper_ref[head], temper)

    pair_copy.wait()
    step = width
    for start in range(0, width, step):
        kv_ref[:, start : start + step] = jnp.dot(
            normed_ref[...], pair_ref[:, start : start + step], preferred_element_type=jnp.float32
        ).astype(jnp.bfloat16)
    normed_last = jnp.dot(pick, normed_ref[...], preferred_element_type=jnp.float32).astype(
        jnp.bfloat16
    )
    flat = caption_ref[...].reshape(tokens, width)
    summed_last = jnp.dot(pick, flat, preferred_element_type=jnp.float32) + jnp.dot(
        pick_position, position_ref[...], preferred_element_type=jnp.float32
    )
    query_copy.wait()
    queries = lax.dot_general(
        normed_last, query_ref[...], NT, preferred_element_type=jnp.float32
    )
    query_norm = temper * lax.rsqrt(split_dot(queries * queries, key_heads) + 1e-06)
    query_high = queries.astype(jnp.bfloat16)
    query_low = (queries - query_high.astype(jnp.float32)).astype(jnp.bfloat16)
    norm_high = query_norm.astype(jnp.bfloat16)
    norm_low = (query_norm - norm_high.astype(jnp.float32)).astype(jnp.bfloat16)

    attended = jnp.zeros((number, wide_inner), jnp.float32)
    parts = 1
    some = tokens // parts
    for part in range(parts):
        rows = slice(part * some, (part + 1) * some)
        spread_part = spread[rows]
        query_tok = jnp.dot(
            spread_part, query_high, preferred_element_type=jnp.float32
        ) + jnp.dot(spread_part, query_low, preferred_element_type=jnp.float32)
        norm_tok = jnp.dot(
            spread_part, norm_high, preferred_element_type=jnp.float32
        ) + jnp.dot(spread_part, norm_low, preferred_element_type=jnp.float32)
        keys = kv_ref[rows, 0:inner].astype(jnp.float32)
        products = split_dot(keys * query_tok, key_heads)
        key_square = split_dot(keys * keys, key_heads)
        scores = products * lax.rsqrt(key_square + 1e-06) * norm_tok
        raised = jnp.where(place_tok[rows] < count_tok[rows], jnp.exp(scores), 0.0)
        raised = raised.reshape(some // length, length, LANES)
        probs = raised / jnp.sum(raised, axis=1, keepdims=True)
        probs = probs.reshape(some, LANES).astype(jnp.bfloat16)
        probs_wide = jnp.dot(probs, value_heads, preferred_element_type=jnp.float32)
        values = kv_ref[rows, width - wide_inner : width].astype(jnp.float32)
        weighed = probs_wide * values
        high = weighed.astype(jnp.bfloat16)
        low = (weighed - high.astype(jnp.float32)).astype(jnp.bfloat16)
        attended = (
            attended
            + jnp.dot(member[:, rows], high, preferred_element_type=jnp.float32)
            + jnp.dot(member[:, rows], low, preferred_element_type=jnp.float32)
        )
    out_copy.wait()
    residual = summed_last + jnp.dot(
        attended.astype(jnp.bfloat16), out_ref[...], preferred_element_type=jnp.float32
    )
    gain_out_copy.wait()
    final = layer_norm(residual, gain_out_ref[...].reshape(1, width)).astype(jnp.bfloat16)
    head_copy.wait()
    pooled = unit_rows(jnp.dot(final, head_ref[...], preferred_element_type=jnp.float32)).astype(
        jnp.bfloat16
    )
    target_copy.wait()
    route = as_half(target_ref[...] == iota((slots, number), 0))
    wide_ref[:, 0:width] = jnp.dot(route, pooled, preferred_element_type=jnp.float32).astype(
        jnp.bfloat16
    )
    label_int = label_col.astype(jnp.int32)
    column = iota((number, AUX), 1)
    aux = jnp.where(
        column == 0,
        label_int // 32,
        jnp.where(column == 1, label_int % 32, jnp.where(column == 2, 1, 0)),
    )
    aux = aux.astype(jnp.float32).astype(jnp.bfloat16)
    wide_ref[:, width : width + AUX] = jnp.dot(
        route, aux, preferred_element_type=jnp.float32
    ).astype(jnp.bfloat16)


def encode(captions, counts, target, label, params, slots):
    position, gain_in, gain_out, query_proj, pair_proj, out_proj, head_proj, temper = params
    number, length, width = captions.shape
    inner = query_proj.shape[1]
    lead = -inner % LANES
    vmem = pl.BlockSpec()
    smem = pl.BlockSpec(memory_space=pltpu.SMEM)
    hbm = pl.BlockSpec(memory_space=pl.ANY)
    return pl.pallas_call(
        tower_kernel,
        out_shape=jax.ShapeDtypeStruct((slots, width + AUX), jnp.bfloat16),
        in_specs=[smem] + [hbm] * 11,
        out_specs=vmem,
        scratch_shapes=[
            pltpu.VMEM((1, number), jnp.int32),
            pltpu.VMEM((1, number), jnp.int32),
            pltpu.VMEM((1, number), jnp.int32),
            pltpu.VMEM((number, length, width), jnp.bfloat16),
            pltpu.VMEM((length, width), jnp.bfloat16),
            pltpu.VMEM((width,), jnp.float32),
            pltpu.VMEM((width,), jnp.float32),
            pltpu.VMEM((inner, width), jnp.bfloat16),
            pltpu.VMEM((width, width), jnp.bfloat16),
            pltpu.VMEM((lead + inner, width), jnp.bfloat16),
            pltpu.VMEM((width, width), jnp.bfloat16),
            pltpu.VMEM((number * length, width), jnp.bfloat16),
            pltpu.VMEM((number * length, width), jnp.bfloat16),
            pltpu.SemaphoreType.DMA((10 + BATCHES,)),
        ],
        compiler_params=pltpu.CompilerParams(vmem_limit_bytes=56 * 1024 * 1024),
        cost_estimate=pl.CostEstimate(
            flops=2 * number * length * width * width,
            bytes_accessed=10_000_000,
            transcendentals=number * length * LANES,
        ),
        name="tower",
    )(
        temper,
        counts.reshape(1, number),
        target.reshape(1, number),
        label.reshape(1, number),
        captions,
        position,
        gain_in,
        gain_out,
        query_proj.T,
        pair_proj,
        out_proj,
        head_proj,
    )


def slope_of(logits, same, live):
    sign = jnp.where(same, 1.0, -1.0)
    return -sign / (1.0 + jnp.exp(sign * logits)) * live


def inverse_norm(values):
    values = values.astype(jnp.float32)
    return lax.rsqrt(jnp.sum(values * values, axis=-1, keepdims=True) + 1e-06)


def aux_rows(aux):
    row, column = iota((8, AUX), 0), iota((8, AUX), 1)
    pick = jnp.where(
        row == 0,
        jnp.where(column == 0, 32.0, jnp.where(column == 1, 1.0, 0.0)),
        jnp.where((row == 1) & (column == 2), 1.0, 0.0),
    ).astype(jnp.bfloat16)
    rows = lax.dot_general(pick, aux, NT, preferred_element_type=jnp.float32)
    return rows[0:1], rows[1:2]


def places(mine_ref):
    mine = mine_ref[0]
    return mine // (XS * CS), mine // CS % XS, mine % CS


def text_parts_kernel(scale_ref, offset_ref, mine_ref, wide_ref, images_ref, parts_ref):
    number, width = images_ref.shape
    count = number // (ZS * CS)
    z, x, _ = places(mine_ref)
    images = images_ref[...]
    text = wide_ref[:, 0:width]
    label, live = aux_rows(wide_ref[:, width:])
    inverse = inverse_norm(images)
    logits = lax.dot_general(images, text, NT, preferred_element_type=jnp.float32)
    logits = (scale_ref[0] * inverse) * logits + offset_ref[0]
    row = iota((number, 1), 0)
    place = (((row // count % ZS) ^ z) * XS + x) * CS + row // (count * ZS)
    index = (place * count + row % count).astype(jnp.float32)
    slopes = (slope_of(logits, label == index, live) * inverse).astype(jnp.bfloat16)
    parts_ref[...] = lax.dot_general(
        slopes, images, TN, preferred_element_type=jnp.float32
    ).astype(jnp.bfloat16)


def image_parts_kernel(scale_ref, offset_ref, mine_ref, wide_ref, images_ref, parts_ref):
    number, width = images_ref.shape
    count = number // ZS
    z, x, core = places(mine_ref)
    images = images_ref[...]
    text = wide_ref[:, 0:width]
    label, live = aux_rows(wide_ref[:, width:])
    logits = lax.dot_general(images, text, NT, preferred_element_type=jnp.float32)
    logits = (scale_ref[0] * inverse_norm(images)) * logits + offset_ref[0]
    row = iota((number, 1), 0)
    place = ((row // count ^ z) * XS + x) * CS + core
    index = (place * count + row % count).astype(jnp.float32)
    slopes = slope_of(logits, label == index, live).astype(jnp.bfloat16)
    parts = jnp.dot(slopes, text, preferred_element_type=jnp.float32).astype(jnp.bfloat16)
    for block in range(ZS):
        first = pl.multiple_of((z ^ block) * count, count)
        parts_ref[pl.ds(first, count), :] = parts[block * count : (block + 1) * count]


def call_parts(kernel, scalars, wide, images, rows, name):
    number, width = images.shape
    smem = pl.BlockSpec(memory_space=pltpu.SMEM)
    vmem = pl.BlockSpec(memory_space=pltpu.VMEM)
    return pl.pallas_call(
        kernel,
        out_shape=jax.ShapeDtypeStruct((rows, width), jnp.bfloat16),
        in_specs=[smem] * len(scalars) + [vmem, vmem],
        out_specs=vmem,
        compiler_params=pltpu.CompilerParams(vmem_limit_bytes=24 * 1024 * 1024),
        cost_estimate=pl.CostEstimate(
            flops=4 * wide.shape[0] * number * width,
            bytes_accessed=4 * number * width,
            transcendentals=wide.shape[0] * number,
        ),
        name=name,
    )(*scalars, wide, images)


def exchange(blocks, groups):
    return lax.all_to_all(
        blocks, "blk", split_axis=0, concat_axis=0, tiled=True, axis_index_groups=groups
    )


def spread_to(rows, groups):
    members = len(groups[0])
    got = exchange(jnp.broadcast_to(rows[None], (members,) + rows.shape), groups)
    return got.reshape(members * rows.shape[0], rows.shape[1])


def groups_of():
    place = lambda z, x, c: (z * XS + x) * CS + c
    lines = [[place(z, x, c) for z in range(ZS)] for x in range(XS) for c in range(CS)]
    rings = [[place(z, x, c) for x in range(XS)] for z in range(ZS) for c in range(CS)]
    pairs = [[place(z, x, c) for c in range(CS)] for z in range(ZS) for x in range(XS)]
    return lines, rings, pairs


def across(rows, bit):
    place = lambda z, x, c: (z * XS + x) * CS + c
    swap = [
        (place(z, x, c), place(z ^ bit, x, c))
        for z in range(ZS)
        for x in range(XS)
        for c in range(CS)
    ]
    return lax.ppermute(rows, "blk", swap)


def both_cores(rows, pairs):
    return lax.all_gather(rows, "blk", axis=0, tiled=True, axis_index_groups=pairs)


def summed_parts(got, scale):
    return scale * jnp.sum(got.astype(jnp.float32), axis=0)


def loss_grads(wide, near, scale, offset, groups):
    lines, rings, pairs = groups
    number, width = near.shape
    count = number // ZS
    slots = wide.shape[0]
    mine = lax.axis_index("blk").reshape(1)
    ring = spread_to(wide, rings)
    text_parts = call_parts(
        text_parts_kernel,
        (scale, offset, mine),
        ring,
        both_cores(near, pairs),
        ring.shape[0],
        "text_parts",
    )
    text_parts, ring = lax.optimization_barrier((text_parts, ring))
    text_got = exchange(text_parts.reshape(-1, slots, width), rings)
    image_parts = call_parts(
        image_parts_kernel,
        (scale, offset, mine),
        both_cores(ring, pairs),
        near,
        number,
        "image_parts",
    )
    text_got, image_parts = lax.optimization_barrier((text_got, image_parts))
    image_got = exchange(image_parts.reshape(-1, count, width), lines)
    return summed_parts(text_got, scale), summed_parts(image_got, scale)


def local(
    captions,
    lengths,
    destination,
    labels,
    images,
    position,
    gain_in,
    gain_out,
    query_proj,
    pair_proj,
    out_proj,
    head_proj,
    temper,
    logit_scale,
    logit_bias,
):
    slots = lax.axis_size("dp")
    params = (position, gain_in, gain_out, query_proj, pair_proj, out_proj, head_proj, temper)
    groups = groups_of()
    own = images[0, 0]
    beside = across(own, 1)
    sent = encode(captions[0, 0], lengths[0, 0], destination[0, 0], labels[0, 0], params, slots)
    two = jnp.concatenate([own, beside])
    sent, two = lax.optimization_barrier((sent, two))
    far = across(two, 2)
    halves = sent.reshape(slots, 2, sent.shape[1] // 2)
    wide = lax.all_to_all(halves, "dp", split_axis=0, concat_axis=0, tiled=True)
    near = jnp.concatenate([two, far])
    wide = wide.reshape(sent.shape)
    text_sum, image_sum = loss_grads(wide, near, logit_scale, logit_bias, groups)
    return text_sum[None, None], image_sum[None, None]


def solution(mesh):
    return jax.shard_map(
        local,
        mesh=mesh,
        in_specs=(
            P("dp", "blk", None, None, None),
            P("dp", "blk", None),
            P("dp", "blk", None),
            P("dp", "blk", None),
            P("dp", "blk", None, None),
            P(),
            P(),
            P(),
            P(),
            P(),
            P(),
            P(),
            P(),
            P(),
            P(),
        ),
        out_specs=(P("dp", "blk", None, None), P("dp", "blk", None, None)),
        check_vma=False,
    )
```

```python
import jax
import jax.numpy as jnp
from jax import lax
from jax.experimental import pallas as pl
from jax.experimental.pallas import tpu as pltpu
from jax.sharding import PartitionSpec as P

CS = 2
XS = 4
ZS = 4
LANES = 128
AUX = 128
BATCHES = 2
NT = (((1,), (1,)), ((), ()))
TN = (((0,), (0,)), ((), ()))


def layer_norm(values, gain):
    center = values - jnp.mean(values, axis=-1, keepdims=True)
    spread = jnp.mean(center * center, axis=-1, keepdims=True)
    return center * lax.rsqrt(spread + 1e-06) * gain


def unit_rows(values):
    return values * lax.rsqrt(jnp.sum(values * values, axis=-1, keepdims=True) + 1e-06)


def split_dot(values, right, dims=(((1,), (0,)), ((), ()))):
    high = values.astype(jnp.bfloat16)
    low = (values - high.astype(jnp.float32)).astype(jnp.bfloat16)
    return lax.dot_general(high, right, dims, preferred_element_type=jnp.float32) + lax.dot_general(
        low, right, dims, preferred_element_type=jnp.float32
    )


def as_half(mask):
    return jnp.where(mask, 1.0, 0.0).astype(jnp.bfloat16)


def iota(shape, dimension):
    return lax.broadcasted_iota(jnp.int32, shape, dimension)


def tower_kernel(
    temper_ref,
    count_hbm,
    target_hbm,
    label_hbm,
    caption_hbm,
    position_hbm,
    gain_in_hbm,
    gain_out_hbm,
    query_hbm,
    pair_hbm,
    out_hbm,
    head_hbm,
    wide_ref,
    count_ref,
    target_ref,
    label_ref,
    caption_ref,
    position_ref,
    gain_in_ref,
    gain_out_ref,
    query_ref,
    pair_ref,
    out_ref,
    head_ref,
    normed_ref,
    kv_ref,
    sems,
):
    number, length, width = caption_ref.shape
    tokens = number * length
    inner = query_hbm.shape[0]
    heads = temper_ref.shape[0]
    size = inner // heads
    lead = out_ref.shape[0] - inner
    slots = wide_ref.shape[0]
    pair_copy = pltpu.make_async_copy(pair_hbm, pair_ref, sems.at[0])
    query_copy = pltpu.make_async_copy(query_hbm, query_ref, sems.at[1])
    out_copy = pltpu.make_async_copy(out_hbm, out_ref.at[pl.ds(lead, inner), :], sems.at[2])
    head_copy = pltpu.make_async_copy(head_hbm, head_ref, sems.at[3])
    group = number // BATCHES
    position_copy = pltpu.make_async_copy(position_hbm, position_ref, sems.at[4])
    gain_in_copy = pltpu.make_async_copy(gain_in_hbm, gain_in_ref, sems.at[5])
    gain_out_copy = pltpu.make_async_copy(gain_out_hbm, gain_out_ref, sems.at[6])
    count_copy = pltpu.make_async_copy(count_hbm, count_ref, sems.at[7])
    target_copy = pltpu.make_async_copy(target_hbm, target_ref, sems.at[8])
    label_copy = pltpu.make_async_copy(label_hbm, label_ref, sems.at[9])
    caption_copies = [
        pltpu.make_async_copy(
            caption_hbm.at[pl.ds(batch * group, group)],
            caption_ref.at[pl.ds(batch * group, group)],
            sems.at[10 + batch],
        )
        for batch in range(BATCHES)
    ]
    position_copy.start()
    gain_in_copy.start()
    for copy in caption_copies:
        copy.start()
    pair_copy.start()
    count_copy.start()
    label_copy.start()
    query_copy.start()
    out_copy.start()
    target_copy.start()
    gain_out_copy.start()
    head_copy.start()
    out_ref[0:lead, :] = jnp.zeros((lead, width), jnp.bfloat16)

    position_copy.wait()
    gain_in_copy.wait()
    gain_in = gain_in_ref[...].reshape(1, width)
    position = position_ref[...].astype(jnp.float32)
    for batch in range(BATCHES):
        start = batch * group
        caption_copies[batch].wait()
        summed = caption_ref[start : start + group].astype(jnp.float32) + position[None]
        normed = layer_norm(summed, gain_in[None]).astype(jnp.bfloat16)
        normed_ref[start * length : (start + group) * length, :] = normed.reshape(
            group * length, width
        )

    count_copy.wait()
    label_copy.wait()
    count_row = jnp.maximum(count_ref[...], 1).astype(jnp.float32)
    label_row = label_ref[...].astype(jnp.float32)
    diagonal = iota((number, number), 0) == iota((number, number), 1)
    count_col = jnp.sum(jnp.where(diagonal, count_row, 0.0), axis=1, keepdims=True)
    label_col = jnp.sum(jnp.where(diagonal, label_row, 0.0), axis=1, keepdims=True)
    last_col = count_col.astype(jnp.int32) - 1
    pick = as_half(iota((number, tokens), 1) == iota((number, tokens), 0) * length + last_col)
    pick_position = as_half(iota((number, length), 1) == last_col)
    member = as_half(iota((number, tokens), 1) // length == iota((number, tokens), 0))
    owner = iota((tokens, number), 0) // length == iota((tokens, number), 1)
    spread = as_half(owner)
    count_tok = jnp.sum(jnp.where(owner, count_row, 0.0), axis=1, keepdims=True)
    place_tok = (iota((tokens, 1), 0) % length).astype(jnp.float32)
    first = iota((inner, LANES), 1) * size
    key_heads = as_half((iota((inner, LANES), 0) >= first) & (iota((inner, LANES), 0) < first + size))
    wide_inner = lead + inner
    first = iota((LANES, wide_inner), 0) * size + lead
    value_heads = as_half(
        (iota((LANES, wide_inner), 1) >= first) & (iota((LANES, wide_inner), 1) < first + size)
    )
    lane = iota((1, LANES), 1)
    temper = jnp.zeros((1, LANES), jnp.float32)
    for head in range(heads):
        temper = jnp.where(lane == head, temper_ref[head], temper)

    pair_copy.wait()
    step = width
    for start in range(0, width, step):
        kv_ref[:, start : start + step] = jnp.dot(
            normed_ref[...], pair_ref[:, start : start + step], preferred_element_type=jnp.float32
        ).astype(jnp.bfloat16)
    normed_last = jnp.dot(pick, normed_ref[...], preferred_element_type=jnp.float32).astype(
        jnp.bfloat16
    )
    flat = caption_ref[...].reshape(tokens, width)
    summed_last = jnp.dot(pick, flat, preferred_element_type=jnp.float32) + jnp.dot(
        pick_position, position_ref[...], preferred_element_type=jnp.float32
    )
    query_copy.wait()
    queries = lax.dot_general(
        normed_last, query_ref[...], NT, preferred_element_type=jnp.float32
    )
    query_norm = temper * lax.rsqrt(split_dot(queries * queries, key_heads) + 1e-06)
    query_high = queries.astype(jnp.bfloat16)
    query_low = (queries - query_high.astype(jnp.float32)).astype(jnp.bfloat16)
    norm_high = query_norm.astype(jnp.bfloat16)
    norm_low = (query_norm - norm_high.astype(jnp.float32)).astype(jnp.bfloat16)

    attended = jnp.zeros((number, wide_inner), jnp.float32)
    parts = 1
    some = tokens // parts
    for part in range(parts):
        rows = slice(part * some, (part + 1) * some)
        spread_part = spread[rows]
        query_tok = jnp.dot(
            spread_part, query_high, preferred_element_type=jnp.float32
        ) + jnp.dot(spread_part, query_low, preferred_element_type=jnp.float32)
        norm_tok = jnp.dot(
            spread_part, norm_high, preferred_element_type=jnp.float32
        ) + jnp.dot(spread_part, norm_low, preferred_element_type=jnp.float32)
        keys = kv_ref[rows, 0:inner].astype(jnp.float32)
        products = split_dot(keys * query_tok, key_heads)
        key_square = split_dot(keys * keys, key_heads)
        scores = products * lax.rsqrt(key_square + 1e-06) * norm_tok
        raised = jnp.where(place_tok[rows] < count_tok[rows], jnp.exp(scores), 0.0)
        raised = raised.reshape(some // length, length, LANES)
        probs = raised / jnp.sum(raised, axis=1, keepdims=True)
        probs = probs.reshape(some, LANES).astype(jnp.bfloat16)
        probs_wide = jnp.dot(probs, value_heads, preferred_element_type=jnp.float32)
        values = kv_ref[rows, width - wide_inner : width].astype(jnp.float32)
        weighed = probs_wide * values
        high = weighed.astype(jnp.bfloat16)
        low = (weighed - high.astype(jnp.float32)).astype(jnp.bfloat16)
        attended = (
            attended
            + jnp.dot(member[:, rows], high, preferred_element_type=jnp.float32)
            + jnp.dot(member[:, rows], low, preferred_element_type=jnp.float32)
        )
    out_copy.wait()
    residual = summed_last + jnp.dot(
        attended.astype(jnp.bfloat16), out_ref[...], preferred_element_type=jnp.float32
    )
    gain_out_copy.wait()
    final = layer_norm(residual, gain_out_ref[...].reshape(1, width)).astype(jnp.bfloat16)
    head_copy.wait()
    pooled = unit_rows(jnp.dot(final, head_ref[...], preferred_element_type=jnp.float32)).astype(
        jnp.bfloat16
    )
    target_copy.wait()
    route = as_half(target_ref[...] == iota((slots, number), 0))
    wide_ref[:, 0:width] = jnp.dot(route, pooled, preferred_element_type=jnp.float32).astype(
        jnp.bfloat16
    )
    label_int = label_col.astype(jnp.int32)
    column = iota((number, AUX), 1)
    aux = jnp.where(
        column == 0,
        label_int // 32,
        jnp.where(column == 1, label_int % 32, jnp.where(column == 2, 1, 0)),
    )
    aux = aux.astype(jnp.float32).astype(jnp.bfloat16)
    wide_ref[:, width : width + AUX] = jnp.dot(
        route, aux, preferred_element_type=jnp.float32
    ).astype(jnp.bfloat16)


def encode(captions, counts, target, label, params, slots):
    position, gain_in, gain_out, query_proj, pair_proj, out_proj, head_proj, temper = params
    number, length, width = captions.shape
    inner = query_proj.shape[1]
    lead = -inner % LANES
    vmem = pl.BlockSpec()
    smem = pl.BlockSpec(memory_space=pltpu.SMEM)
    hbm = pl.BlockSpec(memory_space=pl.ANY)
    return pl.pallas_call(
        tower_kernel,
        out_shape=jax.ShapeDtypeStruct((slots, width + AUX), jnp.bfloat16),
        in_specs=[smem] + [hbm] * 11,
        out_specs=vmem,
        scratch_shapes=[
            pltpu.VMEM((1, number), jnp.int32),
            pltpu.VMEM((1, number), jnp.int32),
            pltpu.VMEM((1, number), jnp.int32),
            pltpu.VMEM((number, length, width), jnp.bfloat16),
            pltpu.VMEM((length, width), jnp.bfloat16),
            pltpu.VMEM((width,), jnp.float32),
            pltpu.VMEM((width,), jnp.float32),
            pltpu.VMEM((inner, width), jnp.bfloat16),
            pltpu.VMEM((width, width), jnp.bfloat16),
            pltpu.VMEM((lead + inner, width), jnp.bfloat16),
            pltpu.VMEM((width, width), jnp.bfloat16),
            pltpu.VMEM((number * length, width), jnp.bfloat16),
            pltpu.VMEM((number * length, width), jnp.bfloat16),
            pltpu.SemaphoreType.DMA((10 + BATCHES,)),
        ],
        compiler_params=pltpu.CompilerParams(vmem_limit_bytes=56 * 1024 * 1024),
        cost_estimate=pl.CostEstimate(
            flops=2 * number * length * width * width,
            bytes_accessed=10_000_000,
            transcendentals=number * length * LANES,
        ),
        name="tower",
    )(
        temper,
        counts.reshape(1, number),
        target.reshape(1, number),
        label.reshape(1, number),
        captions,
        position,
        gain_in,
        gain_out,
        query_proj.T,
        pair_proj,
        out_proj,
        head_proj,
    )


def slope_of(logits, same, live):
    sign = jnp.where(same, 1.0, -1.0)
    return -sign / (1.0 + jnp.exp(sign * logits)) * live


def inverse_norm(values):
    values = values.astype(jnp.float32)
    return lax.rsqrt(jnp.sum(values * values, axis=-1, keepdims=True) + 1e-06)


def aux_rows(aux):
    row, column = iota((8, AUX), 0), iota((8, AUX), 1)
    pick = jnp.where(
        row == 0,
        jnp.where(column == 0, 32.0, jnp.where(column == 1, 1.0, 0.0)),
        jnp.where((row == 1) & (column == 2), 1.0, 0.0),
    ).astype(jnp.bfloat16)
    rows = lax.dot_general(pick, aux, NT, preferred_element_type=jnp.float32)
    return rows[0:1], rows[1:2]


def places(mine_ref):
    mine = mine_ref[0]
    return mine // (XS * CS), mine // CS % XS, mine % CS


def text_parts_kernel(scale_ref, offset_ref, mine_ref, wide_ref, images_ref, parts_ref):
    number, width = images_ref.shape
    count = number // (ZS * CS)
    z, x, _ = places(mine_ref)
    images = images_ref[...]
    text = wide_ref[:, 0:width]
    label, live = aux_rows(wide_ref[:, width:])
    inverse = inverse_norm(images)
    logits = lax.dot_general(images, text, NT, preferred_element_type=jnp.float32)
    logits = (scale_ref[0] * inverse) * logits + offset_ref[0]
    row = iota((number, 1), 0)
    place = (((row // count % ZS) ^ z) * XS + x) * CS + row // (count * ZS)
    index = (place * count + row % count).astype(jnp.float32)
    slopes = (slope_of(logits, label == index, live) * inverse).astype(jnp.bfloat16)
    parts_ref[...] = lax.dot_general(
        slopes, images, TN, preferred_element_type=jnp.float32
    ).astype(jnp.bfloat16)


def image_parts_kernel(scale_ref, offset_ref, mine_ref, wide_ref, images_ref, own_ref, *part_refs):
    number, width = images_ref.shape
    count = number // ZS
    z, x, core = places(mine_ref)
    images = images_ref[...]
    text = wide_ref[:, 0:width]
    label, live = aux_rows(wide_ref[:, width:])
    logits = lax.dot_general(images, text, NT, preferred_element_type=jnp.float32)
    logits = (scale_ref[0] * inverse_norm(images)) * logits + offset_ref[0]
    row = iota((number, 1), 0)
    place = ((row // count ^ z) * XS + x) * CS + core
    index = (place * count + row % count).astype(jnp.float32)
    slopes = slope_of(logits, label == index, live).astype(jnp.bfloat16)
    parts = jnp.dot(slopes, text, preferred_element_type=jnp.float32)
    own_ref[...] = parts[0:count]
    for block, part_ref in enumerate(part_refs, 1):
        part_ref[...] = parts[block * count : (block + 1) * count].astype(jnp.bfloat16)


def call_parts(kernel, scalars, wide, images, outs, name):
    number, width = images.shape
    smem = pl.BlockSpec(memory_space=pltpu.SMEM)
    vmem = pl.BlockSpec(memory_space=pltpu.VMEM)
    return pl.pallas_call(
        kernel,
        out_shape=[jax.ShapeDtypeStruct((rows, width), dtype) for rows, dtype in outs],
        in_specs=[smem] * len(scalars) + [vmem, vmem],
        out_specs=[vmem] * len(outs),
        compiler_params=pltpu.CompilerParams(vmem_limit_bytes=24 * 1024 * 1024),
        cost_estimate=pl.CostEstimate(
            flops=4 * wide.shape[0] * number * width,
            bytes_accessed=4 * number * width,
            transcendentals=wide.shape[0] * number,
        ),
        name=name,
    )(*scalars, wide, images)


def exchange(blocks, groups):
    return lax.all_to_all(
        blocks, "blk", split_axis=0, concat_axis=0, tiled=True, axis_index_groups=groups
    )


def spread_to(rows, groups):
    members = len(groups[0])
    got = exchange(jnp.broadcast_to(rows[None], (members,) + rows.shape), groups)
    return got.reshape(members * rows.shape[0], rows.shape[1])


def groups_of():
    place = lambda z, x, c: (z * XS + x) * CS + c
    lines = [[place(z, x, c) for z in range(ZS)] for x in range(XS) for c in range(CS)]
    rings = [[place(z, x, c) for x in range(XS)] for z in range(ZS) for c in range(CS)]
    pairs = [[place(z, x, c) for c in range(CS)] for z in range(ZS) for x in range(XS)]
    return lines, rings, pairs


def across(rows, bit):
    place = lambda z, x, c: (z * XS + x) * CS + c
    swap = [
        (place(z, x, c), place(z ^ bit, x, c))
        for z in range(ZS)
        for x in range(XS)
        for c in range(CS)
    ]
    return lax.ppermute(rows, "blk", swap)


def both_cores(rows, pairs):
    return lax.all_gather(rows, "blk", axis=0, tiled=True, axis_index_groups=pairs)


def summed_parts(got, scale):
    return scale * jnp.sum(got.astype(jnp.float32), axis=0)


def loss_grads(wide, near, scale, offset, groups):
    lines, rings, pairs = groups
    number, width = near.shape
    count = number // ZS
    slots = wide.shape[0]
    mine = lax.axis_index("blk").reshape(1)
    ring = spread_to(wide, rings)
    (text_parts,) = call_parts(
        text_parts_kernel,
        (scale, offset, mine),
        ring,
        both_cores(near, pairs),
        [(ring.shape[0], jnp.bfloat16)],
        "text_parts",
    )
    text_parts, ring = lax.optimization_barrier((text_parts, ring))
    text_got = exchange(text_parts.reshape(-1, slots, width), rings)
    image_sum, *image_parts = call_parts(
        image_parts_kernel,
        (scale, offset, mine),
        both_cores(ring, pairs),
        near,
        [(count, jnp.float32)] + [(count, jnp.bfloat16)] * (ZS - 1),
        "image_parts",
    )
    farthest = across(image_parts.pop(), ZS - 1)
    text_got, image_parts = lax.optimization_barrier((text_got, image_parts))
    got = [across(part, bits) for bits, part in enumerate(image_parts, 1)]
    for part in [farthest] + got[::-1]:
        image_sum = image_sum + part.astype(jnp.float32)
    return summed_parts(text_got, scale), scale * image_sum


def local(
    captions,
    lengths,
    destination,
    labels,
    images,
    position,
    gain_in,
    gain_out,
    query_proj,
    pair_proj,
    out_proj,
    head_proj,
    temper,
    logit_scale,
    logit_bias,
):
    slots = lax.axis_size("dp")
    params = (position, gain_in, gain_out, query_proj, pair_proj, out_proj, head_proj, temper)
    groups = groups_of()
    own = images[0, 0]
    beside = across(own, 1)
    sent = encode(captions[0, 0], lengths[0, 0], destination[0, 0], labels[0, 0], params, slots)
    two = jnp.concatenate([own, beside])
    sent, two = lax.optimization_barrier((sent, two))
    far = across(two, 2)
    halves = sent.reshape(slots, 2, sent.shape[1] // 2)
    wide = lax.all_to_all(halves, "dp", split_axis=0, concat_axis=0, tiled=True)
    near = jnp.concatenate([two, far])
    wide = wide.reshape(sent.shape)
    text_sum, image_sum = loss_grads(wide, near, logit_scale, logit_bias, groups)
    return text_sum[None, None], image_sum[None, None]


def solution(mesh):
    return jax.shard_map(
        local,
        mesh=mesh,
        in_specs=(
            P("dp", "blk", None, None, None),
            P("dp", "blk", None),
            P("dp", "blk", None),
            P("dp", "blk", None),
            P("dp", "blk", None, None),
            P(),
            P(),
            P(),
            P(),
            P(),
            P(),
            P(),
            P(),
            P(),
            P(),
        ),
        out_specs=(P("dp", "blk", None, None), P("dp", "blk", None, None)),
        check_vma=False,
    )
```

```python
import jax
import jax.numpy as jnp
from jax import lax
from jax.experimental import pallas as pl
from jax.experimental.pallas import tpu as pltpu
from jax.sharding import PartitionSpec as P

CS = 2
XS = 4
ZS = 4
LANES = 128
AUX = 128
BATCHES = 2
NT = (((1,), (1,)), ((), ()))
TN = (((0,), (0,)), ((), ()))


def layer_norm(values, gain):
    center = values - jnp.mean(values, axis=-1, keepdims=True)
    spread = jnp.mean(center * center, axis=-1, keepdims=True)
    return center * lax.rsqrt(spread + 1e-06) * gain


def unit_rows(values):
    return values * lax.rsqrt(jnp.sum(values * values, axis=-1, keepdims=True) + 1e-06)


def split_dot(values, right, dims=(((1,), (0,)), ((), ()))):
    high = values.astype(jnp.bfloat16)
    low = (values - high.astype(jnp.float32)).astype(jnp.bfloat16)
    return lax.dot_general(high, right, dims, preferred_element_type=jnp.float32) + lax.dot_general(
        low, right, dims, preferred_element_type=jnp.float32
    )


def as_half(mask):
    return jnp.where(mask, 1.0, 0.0).astype(jnp.bfloat16)


def iota(shape, dimension):
    return lax.broadcasted_iota(jnp.int32, shape, dimension)


def tower_kernel(
    temper_ref,
    count_hbm,
    target_hbm,
    label_hbm,
    caption_hbm,
    position_hbm,
    gain_in_hbm,
    gain_out_hbm,
    query_hbm,
    pair_hbm,
    out_hbm,
    head_hbm,
    wide_ref,
    count_ref,
    target_ref,
    label_ref,
    caption_ref,
    position_ref,
    gain_in_ref,
    gain_out_ref,
    query_ref,
    pair_ref,
    out_ref,
    head_ref,
    normed_ref,
    kv_ref,
    sems,
):
    number, length, width = caption_ref.shape
    tokens = number * length
    inner = query_hbm.shape[0]
    heads = temper_ref.shape[0]
    size = inner // heads
    lead = out_ref.shape[0] - inner
    slots = wide_ref.shape[0]
    pair_copy = pltpu.make_async_copy(pair_hbm, pair_ref, sems.at[0])
    query_copy = pltpu.make_async_copy(query_hbm, query_ref, sems.at[1])
    out_copy = pltpu.make_async_copy(out_hbm, out_ref.at[pl.ds(lead, inner), :], sems.at[2])
    head_copy = pltpu.make_async_copy(head_hbm, head_ref, sems.at[3])
    group = number // BATCHES
    position_copy = pltpu.make_async_copy(position_hbm, position_ref, sems.at[4])
    gain_in_copy = pltpu.make_async_copy(gain_in_hbm, gain_in_ref, sems.at[5])
    gain_out_copy = pltpu.make_async_copy(gain_out_hbm, gain_out_ref, sems.at[6])
    count_copy = pltpu.make_async_copy(count_hbm, count_ref, sems.at[7])
    target_copy = pltpu.make_async_copy(target_hbm, target_ref, sems.at[8])
    label_copy = pltpu.make_async_copy(label_hbm, label_ref, sems.at[9])
    caption_copies = [
        pltpu.make_async_copy(
            caption_hbm.at[pl.ds(batch * group, group)],
            caption_ref.at[pl.ds(batch * group, group)],
            sems.at[10 + batch],
        )
        for batch in range(BATCHES)
    ]
    position_copy.start()
    gain_in_copy.start()
    for copy in caption_copies:
        copy.start()
    pair_copy.start()
    count_copy.start()
    label_copy.start()
    query_copy.start()
    out_copy.start()
    target_copy.start()
    gain_out_copy.start()
    head_copy.start()
    out_ref[0:lead, :] = jnp.zeros((lead, width), jnp.bfloat16)

    position_copy.wait()
    gain_in_copy.wait()
    gain_in = gain_in_ref[...].reshape(1, width)
    position = position_ref[...].astype(jnp.float32)
    for batch in range(BATCHES):
        start = batch * group
        caption_copies[batch].wait()
        summed = caption_ref[start : start + group].astype(jnp.float32) + position[None]
        normed = layer_norm(summed, gain_in[None]).astype(jnp.bfloat16)
        normed_ref[start * length : (start + group) * length, :] = normed.reshape(
            group * length, width
        )

    count_copy.wait()
    label_copy.wait()
    count_row = jnp.maximum(count_ref[...], 1).astype(jnp.float32)
    label_row = label_ref[...].astype(jnp.float32)
    diagonal = iota((number, number), 0) == iota((number, number), 1)
    count_col = jnp.sum(jnp.where(diagonal, count_row, 0.0), axis=1, keepdims=True)
    label_col = jnp.sum(jnp.where(diagonal, label_row, 0.0), axis=1, keepdims=True)
    last_col = count_col.astype(jnp.int32) - 1
    pick = as_half(iota((number, tokens), 1) == iota((number, tokens), 0) * length + last_col)
    pick_position = as_half(iota((number, length), 1) == last_col)
    member = as_half(iota((number, tokens), 1) // length == iota((number, tokens), 0))
    owner = iota((tokens, number), 0) // length == iota((tokens, number), 1)
    spread = as_half(owner)
    count_tok = jnp.sum(jnp.where(owner, count_row, 0.0), axis=1, keepdims=True)
    place_tok = (iota((tokens, 1), 0) % length).astype(jnp.float32)
    first = iota((inner, LANES), 1) * size
    key_heads = as_half((iota((inner, LANES), 0) >= first) & (iota((inner, LANES), 0) < first + size))
    wide_inner = lead + inner
    first = iota((LANES, wide_inner), 0) * size + lead
    value_heads = as_half(
        (iota((LANES, wide_inner), 1) >= first) & (iota((LANES, wide_inner), 1) < first + size)
    )
    lane = iota((1, LANES), 1)
    temper = jnp.zeros((1, LANES), jnp.float32)
    for head in range(heads):
        temper = jnp.where(lane == head, temper_ref[head], temper)

    pair_copy.wait()
    step = width
    for start in range(0, width, step):
        kv_ref[:, start : start + step] = jnp.dot(
            normed_ref[...], pair_ref[:, start : start + step], preferred_element_type=jnp.float32
        ).astype(jnp.bfloat16)
    normed_last = jnp.dot(pick, normed_ref[...], preferred_element_type=jnp.float32).astype(
        jnp.bfloat16
    )
    flat = caption_ref[...].reshape(tokens, width)
    summed_last = jnp.dot(pick, flat, preferred_element_type=jnp.float32) + jnp.dot(
        pick_position, position_ref[...], preferred_element_type=jnp.float32
    )
    query_copy.wait()
    queries = lax.dot_general(
        normed_last, query_ref[...], NT, preferred_element_type=jnp.float32
    )
    query_norm = temper * lax.rsqrt(split_dot(queries * queries, key_heads) + 1e-06)
    query_high = queries.astype(jnp.bfloat16)
    query_low = (queries - query_high.astype(jnp.float32)).astype(jnp.bfloat16)
    norm_high = query_norm.astype(jnp.bfloat16)
    norm_low = (query_norm - norm_high.astype(jnp.float32)).astype(jnp.bfloat16)

    attended = jnp.zeros((number, wide_inner), jnp.float32)
    parts = 1
    some = tokens // parts
    for part in range(parts):
        rows = slice(part * some, (part + 1) * some)
        spread_part = spread[rows]
        query_tok = jnp.dot(
            spread_part, query_high, preferred_element_type=jnp.float32
        ) + jnp.dot(spread_part, query_low, preferred_element_type=jnp.float32)
        norm_tok = jnp.dot(
            spread_part, norm_high, preferred_element_type=jnp.float32
        ) + jnp.dot(spread_part, norm_low, preferred_element_type=jnp.float32)
        keys = kv_ref[rows, 0:inner].astype(jnp.float32)
        products = split_dot(keys * query_tok, key_heads)
        key_square = split_dot(keys * keys, key_heads)
        scores = products * lax.rsqrt(key_square + 1e-06) * norm_tok
        raised = jnp.where(place_tok[rows] < count_tok[rows], jnp.exp(scores), 0.0)
        raised = raised.reshape(some // length, length, LANES)
        probs = raised / jnp.sum(raised, axis=1, keepdims=True)
        probs = probs.reshape(some, LANES).astype(jnp.bfloat16)
        probs_wide = jnp.dot(probs, value_heads, preferred_element_type=jnp.float32)
        values = kv_ref[rows, width - wide_inner : width].astype(jnp.float32)
        weighed = probs_wide * values
        high = weighed.astype(jnp.bfloat16)
        low = (weighed - high.astype(jnp.float32)).astype(jnp.bfloat16)
        attended = (
            attended
            + jnp.dot(member[:, rows], high, preferred_element_type=jnp.float32)
            + jnp.dot(member[:, rows], low, preferred_element_type=jnp.float32)
        )
    out_copy.wait()
    residual = summed_last + jnp.dot(
        attended.astype(jnp.bfloat16), out_ref[...], preferred_element_type=jnp.float32
    )
    gain_out_copy.wait()
    final = layer_norm(residual, gain_out_ref[...].reshape(1, width)).astype(jnp.bfloat16)
    head_copy.wait()
    pooled = unit_rows(jnp.dot(final, head_ref[...], preferred_element_type=jnp.float32)).astype(
        jnp.bfloat16
    )
    target_copy.wait()
    route = as_half(target_ref[...] == iota((slots, number), 0))
    label_int = label_col.astype(jnp.int32)
    column = iota((number, AUX), 1)
    aux = jnp.where(
        column == 0,
        label_int // 32,
        jnp.where(column == 1, label_int % 32, jnp.where(column == 2, 1, 0)),
    )
    aux = aux.astype(jnp.float32).astype(jnp.bfloat16)
    half = wide_ref.shape[2]
    tail = jnp.concatenate([pooled[:, half:], aux], axis=1)
    for side, rows in enumerate((pooled[:, :half], tail)):
        wide_ref[:, side, :] = jnp.dot(route, rows, preferred_element_type=jnp.float32).astype(
            jnp.bfloat16
        )


def encode(captions, counts, target, label, params, slots):
    position, gain_in, gain_out, query_proj, pair_proj, out_proj, head_proj, temper = params
    number, length, width = captions.shape
    inner = query_proj.shape[1]
    lead = -inner % LANES
    vmem = pl.BlockSpec()
    smem = pl.BlockSpec(memory_space=pltpu.SMEM)
    hbm = pl.BlockSpec(memory_space=pl.ANY)
    return pl.pallas_call(
        tower_kernel,
        out_shape=jax.ShapeDtypeStruct((slots, 2, (width + AUX) // 2), jnp.bfloat16),
        in_specs=[smem] + [hbm] * 11,
        out_specs=vmem,
        scratch_shapes=[
            pltpu.VMEM((1, number), jnp.int32),
            pltpu.VMEM((1, number), jnp.int32),
            pltpu.VMEM((1, number), jnp.int32),
            pltpu.VMEM((number, length, width), jnp.bfloat16),
            pltpu.VMEM((length, width), jnp.bfloat16),
            pltpu.VMEM((width,), jnp.float32),
            pltpu.VMEM((width,), jnp.float32),
            pltpu.VMEM((inner, width), jnp.bfloat16),
            pltpu.VMEM((width, width), jnp.bfloat16),
            pltpu.VMEM((lead + inner, width), jnp.bfloat16),
            pltpu.VMEM((width, width), jnp.bfloat16),
            pltpu.VMEM((number * length, width), jnp.bfloat16),
            pltpu.VMEM((number * length, width), jnp.bfloat16),
            pltpu.SemaphoreType.DMA((10 + BATCHES,)),
        ],
        compiler_params=pltpu.CompilerParams(vmem_limit_bytes=56 * 1024 * 1024),
        cost_estimate=pl.CostEstimate(
            flops=2 * number * length * width * width,
            bytes_accessed=10_000_000,
            transcendentals=number * length * LANES,
        ),
        name="tower",
    )(
        temper,
        counts.reshape(1, number),
        target.reshape(1, number),
        label.reshape(1, number),
        captions,
        position,
        gain_in,
        gain_out,
        query_proj.T,
        pair_proj,
        out_proj,
        head_proj,
    )


def slope_of(logits, same, live):
    sign = jnp.where(same, 1.0, -1.0)
    return -sign / (1.0 + jnp.exp(sign * logits)) * live


def inverse_norm(values):
    values = values.astype(jnp.float32)
    return lax.rsqrt(jnp.sum(values * values, axis=-1, keepdims=True) + 1e-06)


def aux_rows(aux):
    row, column = iota((8, AUX), 0), iota((8, AUX), 1)
    pick = jnp.where(
        row == 0,
        jnp.where(column == 0, 32.0, jnp.where(column == 1, 1.0, 0.0)),
        jnp.where((row == 1) & (column == 2), 1.0, 0.0),
    ).astype(jnp.bfloat16)
    rows = lax.dot_general(pick, aux, NT, preferred_element_type=jnp.float32)
    return rows[0:1], rows[1:2]


def places(mine_ref):
    mine = mine_ref[0]
    return mine // (XS * CS), mine // CS % XS, mine % CS


def text_parts_kernel(scale_ref, offset_ref, mine_ref, wide_ref, images_ref, parts_ref):
    number, width = images_ref.shape
    count = number // (ZS * CS)
    z, x, _ = places(mine_ref)
    images = images_ref[...]
    text = wide_ref[:, 0:width]
    label, live = aux_rows(wide_ref[:, width:])
    inverse = inverse_norm(images)
    logits = lax.dot_general(images, text, NT, preferred_element_type=jnp.float32)
    logits = (scale_ref[0] * inverse) * logits + offset_ref[0]
    row = iota((number, 1), 0)
    place = (((row // count % ZS) ^ z) * XS + x) * CS + row // (count * ZS)
    index = (place * count + row % count).astype(jnp.float32)
    slopes = (slope_of(logits, label == index, live) * inverse).astype(jnp.bfloat16)
    parts_ref[...] = lax.dot_general(
        slopes, images, TN, preferred_element_type=jnp.float32
    ).astype(jnp.bfloat16)


def image_parts_kernel(scale_ref, offset_ref, mine_ref, wide_ref, images_ref, own_ref, *part_refs):
    number, width = images_ref.shape
    count = number // ZS
    z, x, core = places(mine_ref)
    images = images_ref[...]
    text = wide_ref[:, 0:width]
    label, live = aux_rows(wide_ref[:, width:])
    logits = lax.dot_general(images, text, NT, preferred_element_type=jnp.float32)
    logits = (scale_ref[0] * inverse_norm(images)) * logits + offset_ref[0]
    row = iota((number, 1), 0)
    place = ((row // count ^ z) * XS + x) * CS + core
    index = (place * count + row % count).astype(jnp.float32)
    slopes = slope_of(logits, label == index, live).astype(jnp.bfloat16)
    parts = jnp.dot(slopes, text, preferred_element_type=jnp.float32)
    own_ref[...] = parts[0:count]
    for block, part_ref in enumerate(part_refs, 1):
        part_ref[...] = parts[block * count : (block + 1) * count].astype(jnp.bfloat16)


def call_parts(kernel, scalars, wide, images, outs, name):
    number, width = images.shape
    smem = pl.BlockSpec(memory_space=pltpu.SMEM)
    vmem = pl.BlockSpec(memory_space=pltpu.VMEM)
    return pl.pallas_call(
        kernel,
        out_shape=[jax.ShapeDtypeStruct((rows, width), dtype) for rows, dtype in outs],
        in_specs=[smem] * len(scalars) + [vmem, vmem],
        out_specs=[vmem] * len(outs),
        compiler_params=pltpu.CompilerParams(vmem_limit_bytes=24 * 1024 * 1024),
        cost_estimate=pl.CostEstimate(
            flops=4 * wide.shape[0] * number * width,
            bytes_accessed=4 * number * width,
            transcendentals=wide.shape[0] * number,
        ),
        name=name,
    )(*scalars, wide, images)


def exchange(blocks, groups):
    return lax.all_to_all(
        blocks, "blk", split_axis=0, concat_axis=0, tiled=True, axis_index_groups=groups
    )


def spread_to(rows, groups):
    members = len(groups[0])
    got = exchange(jnp.broadcast_to(rows[None], (members,) + rows.shape), groups)
    return got.reshape(members * rows.shape[0], rows.shape[1])


def groups_of():
    place = lambda z, x, c: (z * XS + x) * CS + c
    lines = [[place(z, x, c) for z in range(ZS)] for x in range(XS) for c in range(CS)]
    rings = [[place(z, x, c) for x in range(XS)] for z in range(ZS) for c in range(CS)]
    pairs = [[place(z, x, c) for c in range(CS)] for z in range(ZS) for x in range(XS)]
    return lines, rings, pairs


def across(rows, bit):
    place = lambda z, x, c: (z * XS + x) * CS + c
    swap = [
        (place(z, x, c), place(z ^ bit, x, c))
        for z in range(ZS)
        for x in range(XS)
        for c in range(CS)
    ]
    return lax.ppermute(rows, "blk", swap)


def both_cores(rows, pairs):
    return lax.all_gather(rows, "blk", axis=0, tiled=True, axis_index_groups=pairs)


def summed_parts(got, scale):
    return scale * jnp.sum(got.astype(jnp.float32), axis=0)


def loss_grads(wide, near, scale, offset, groups):
    lines, rings, pairs = groups
    number, width = near.shape
    count = number // ZS
    slots = wide.shape[0]
    mine = lax.axis_index("blk").reshape(1)
    ring = spread_to(wide, rings)
    (text_parts,) = call_parts(
        text_parts_kernel,
        (scale, offset, mine),
        ring,
        both_cores(near, pairs),
        [(ring.shape[0], jnp.bfloat16)],
        "text_parts",
    )
    text_parts, ring = lax.optimization_barrier((text_parts, ring))
    text_got = exchange(text_parts.reshape(-1, slots, width), rings)
    image_sum, *image_parts = call_parts(
        image_parts_kernel,
        (scale, offset, mine),
        both_cores(ring, pairs),
        near,
        [(count, jnp.float32)] + [(count, jnp.bfloat16)] * (ZS - 1),
        "image_parts",
    )
    farthest = across(image_parts.pop(), ZS - 1)
    text_got, image_parts = lax.optimization_barrier((text_got, image_parts))
    got = [across(part, bits) for bits, part in enumerate(image_parts, 1)]
    for part in [farthest] + got[::-1]:
        image_sum = image_sum + part.astype(jnp.float32)
    return summed_parts(text_got, scale), scale * image_sum


def local(
    captions,
    lengths,
    destination,
    labels,
    images,
    position,
    gain_in,
    gain_out,
    query_proj,
    pair_proj,
    out_proj,
    head_proj,
    temper,
    logit_scale,
    logit_bias,
):
    slots = lax.axis_size("dp")
    params = (position, gain_in, gain_out, query_proj, pair_proj, out_proj, head_proj, temper)
    groups = groups_of()
    own = images[0, 0]
    beside = across(own, 1)
    sent = encode(captions[0, 0], lengths[0, 0], destination[0, 0], labels[0, 0], params, slots)
    two = jnp.concatenate([own, beside])
    sent, two = lax.optimization_barrier((sent, two))
    far = across(two, 2)
    wide = lax.all_to_all(sent, "dp", split_axis=0, concat_axis=0, tiled=True)
    near = jnp.concatenate([two, far])
    wide = wide.reshape(slots, -1)
    text_sum, image_sum = loss_grads(wide, near, logit_scale, logit_bias, groups)
    return text_sum[None, None], image_sum[None, None]


def solution(mesh):
    return jax.shard_map(
        local,
        mesh=mesh,
        in_specs=(
            P("dp", "blk", None, None, None),
            P("dp", "blk", None),
            P("dp", "blk", None),
            P("dp", "blk", None),
            P("dp", "blk", None, None),
            P(),
            P(),
            P(),
            P(),
            P(),
            P(),
            P(),
            P(),
            P(),
            P(),
        ),
        out_specs=(P("dp", "blk", None, None), P("dp", "blk", None, None)),
        check_vma=False,
    )
```
